512 devices in a mesh: row: 16 (over y, core), col: 32 (over z, x).
Axes of the slice: x: 4, y: 8, z: 8, core: 2. Of those that a mesh axis runs over, the one named last changes fastest.
Arguments:
- amplitudes: bfloat16 [4096, 8192], P('row', 'col'), may hold values from -6 to 6
- drive: float32 [4096, 8192], P('row', 'col'), may hold values from -6 to 6
- pair_irrep: int32 [8192], replicated, may hold values from 0 to 7, as said below
- occ_irrep: int32 [4096], replicated, may hold values from 0 to 7
- ladder_ints: bfloat16 [8192, 8192], P('row', 'col'), may hold values from -0.1875 to 0.1875
- hole_ints: bfloat16 [4096, 4096], P('row'), may hold values from -0.25 to 0.25, as said below
- occ_energy: float32 [64], replicated, may hold values from -1.5 to -0.5
- pair_energy: float32 [8192], P('col'), may hold values from 1 to 3
Outputs:
- residual: float32 [4096, 8192], P('row', 'col')
- updated: bfloat16 [4096, 8192], P('row', 'col')
The draws below stay inside these ranges and needn't reach their ends.
Inputs may be any that keep to these rules, and one draw needn't show every extreme that they name: hole_ints is symmetric: hole_ints[ij, kl] == hole_ints[kl, ij]. `pair_irrep`: any irrep may hold any share of the virtual pairs, all of them included.
All inputs are finite; a program needn't handle non-finite values.
Results may differ from the reference program's by a relative error of at most 0.001.
Values may be sent and summed in bfloat16 or wider, within the bound.
No kernel may reach another device: no remote copies, remote signals or barrier semaphores. Data moves between devices by JAX's collectives and lax.ppermute only.
A program may use at most 64 MiB of HBM per device.

```python
import jax
import jax.numpy as jnp

NOCC = 64
IRREPS = 8
OP = 4096
K = 8192
N_ROW = 16


def draw_hole_ints(key, part):
    key = jax.random.fold_in(key, 11)
    base_draw = jax.random.normal(key, (OP, OP), jnp.float32)
    scale_factor = jnp.sqrt(jnp.float32(IRREPS) / (2.0 * OP))
    summed = (base_draw + base_draw.T) * scale_factor
    return jnp.clip(summed, -0.25, 0.25).astype(jnp.bfloat16)


def orbital_labels(weight_key, pick_key):
    weights = jax.random.randint(weight_key, (IRREPS,), 1, 17)
    bounds = jnp.cumsum(weights).astype(jnp.int32)
    picks = jax.random.randint(pick_key, (K,), 0, bounds[IRREPS - 1])
    return jnp.sum((picks[:, None] >= bounds[None, :]).astype(jnp.int32), axis=1).astype(jnp.int32)


def draw_pair_irrep(key, part):
    key = jax.random.fold_in(key, 5)
    subkeys = jax.random.split(key, 6)
    first_orb = orbital_labels(subkeys[0], subkeys[1])
    second_orb = orbital_labels(subkeys[2], subkeys[3])
    labels = jnp.bitwise_xor(first_orb, second_orb)
    block_len = K // N_ROW
    chosen = jax.random.randint(subkeys[4], (), 0, N_ROW)
    filler = jax.random.randint(subkeys[5], (), 0, IRREPS)
    positions = jnp.arange(K, dtype=jnp.int32)
    labels = jnp.where(positions // block_len == chosen, filler, labels)
    return labels.astype(jnp.int32)


def plant(drawn, key, least, largest):
    longest = drawn.shape.index(max(drawn.shape))
    spots = []
    for shift in (0, 1):
        where = [jax.random.randint(jax.random.fold_in(key, axis), (), 0, length) for axis, length in enumerate(drawn.shape)]
        where[longest] = (where[longest] + shift) % drawn.shape[longest]
        spots.append(tuple(where))
    return drawn.at[spots[0]].set(least).at[spots[1]].set(largest)


def shard_levels(stream_key, dims, pieces, low, largest):
    def one(dim, parts):
        draws = jax.random.uniform(jax.random.fold_in(jax.random.fold_in(stream_key, 6), dim), (parts,), jnp.float32, low / len(pieces), largest / len(pieces))
        return jnp.repeat(jnp.exp(draws), dims[dim] // parts).reshape((-1,) + (1,) * (len(dims) - dim - 1))

    factor_of = one(*pieces[0])
    for cut in pieces[1:]:
        factor_of = factor_of * one(*cut)
    return factor_of


def normal_values(key, extent, width, most, pieces=(), kind=jnp.bfloat16):
    level = shard_levels(key, extent, pieces, -0.22, 0.18) if pieces else 1.0
    drawn = jax.random.normal(key, extent, jnp.float32) * width * level
    return jnp.minimum(jnp.maximum(drawn, -most), most).astype(kind)


def setup_inputs(seed: int = 0) -> dict:
    key_of = jax.random.split(jax.random.key(seed), 9)
    amplitudes = normal_values(key_of[0], (OP, K), 1.0, 6.0, ((0, 16), (1, 32)))
    drive = normal_values(key_of[1], (OP, K), 1.0, 6.0, ((0, 16), (1, 32)), jnp.float32)
    pair_irrep = draw_pair_irrep(jax.random.fold_in(key_of[8], 71), 0)
    occ_irrep = plant(jax.random.randint(key_of[3], (OP,), 0, IRREPS), jax.random.fold_in(key_of[3], 1), 0, IRREPS - 1).astype(jnp.int32)
    ladder_ints = normal_values(key_of[4], (K, K), (K // IRREPS) ** -0.5, 0.1875, ((0, 16), (1, 32)))
    hole_ints = draw_hole_ints(jax.random.fold_in(key_of[8], 71), 0)
    occ_energy = jnp.clip(jax.random.uniform(key_of[6], (NOCC,), jnp.float32, -1.5, -0.5), -1.5, -0.5)
    pair_energy = jnp.clip(1.0 + 2.0 * jax.random.uniform(key_of[7], (K,), jnp.float32) ** shard_levels(key_of[7], (K,), ((0, 32),), -0.2, 0.2), 1.0, 3.0)
    return dict(amplitudes=amplitudes, drive=drive, pair_irrep=pair_irrep, occ_irrep=occ_irrep, ladder_ints=ladder_ints, hole_ints=hole_ints, occ_energy=occ_energy, pair_energy=pair_energy)


def reference(amplitudes, drive, pair_irrep, occ_irrep, ladder_ints, hole_ints, occ_energy, pair_energy):
    pair_keep = pair_irrep[:, None] == pair_irrep[None, :]
    ladder_sym = jnp.where(pair_keep, ladder_ints, jnp.zeros_like(ladder_ints))
    occ_keep = occ_irrep[:, None] == occ_irrep[None, :]
    hole_sym = jnp.where(occ_keep, hole_ints, jnp.zeros_like(hole_ints))
    particle = jnp.dot(amplitudes, ladder_sym, preferred_element_type=jnp.float32)
    hole_part = jnp.dot(hole_sym, amplitudes, preferred_element_type=jnp.float32)
    residual = drive + particle + hole_part
    pair_occ = (occ_energy[:, None] + occ_energy[None, :]).reshape(-1)
    denominator = pair_energy[None, :] - pair_occ[:, None]
    updated = (amplitudes.astype(jnp.float32) - residual / denominator).astype(jnp.bfloat16)
    return residual, updated
```

```python
import jax
import jax.numpy as jnp
from jax import lax
from jax.experimental import pallas as pl
from jax.experimental.pallas import tpu as pltpu
from jax.sharding import Mesh, PartitionSpec as P

NY, NCORE, NZ, NX = 8, 2, 8, 4
BF16, F32 = jnp.bfloat16, jnp.float32


def shift(n, by):
    return [(i, (i + by) % n) for i in range(n)]


def place_kernel(where_ref, p0, p1, p2, p3, out_ref, sems):
    copies = []
    for j, piece in enumerate((p0, p1, p2, p3)):
        slot = lax.rem(where_ref[1] + j, NX)
        copies.append(pltpu.make_async_copy(piece, out_ref.at[slot], sems.at[j]))
    for copy in copies:
        copy.start()
    for copy in copies:
        copy.wait()


def place(where, pieces):
    return pl.pallas_call(
        place_kernel,
        out_shape=jax.ShapeDtypeStruct((NX,) + pieces[0].shape, BF16),
        in_specs=[pl.BlockSpec(memory_space=pltpu.SMEM)]
        + [pl.BlockSpec(memory_space=pl.ANY)] * NX,
        out_specs=pl.BlockSpec(memory_space=pl.ANY),
        scratch_shapes=[pltpu.SemaphoreType.DMA((NX,))],
        cost_estimate=pl.CostEstimate(flops=0, bytes_accessed=1 << 20, transcendentals=0),
    )(where, *pieces)


def final_kernel(
    where_ref, gathered, own, f1, f2, f3, f4, b1, b2, b3, b4, hole, amps, drive, own_energy, pair_energy,
    residual_ref, updated_ref, rows_v, amps_v, acc, row_sems, amp_sems,
):
    z = where_ref[0]
    amp_copies = []

    def bring(src, slot, lo, count):
        dst = amps_v.at[slot, pl.ds(lo, count)]
        amp_copies.append(pltpu.make_async_copy(src, dst, amp_sems.at[len(amp_copies)]))
        amp_copies[-1].start()

    row_copies = [
        pltpu.make_async_copy(gathered.at[r], rows_v.at[r], row_sems.at[r])
        for r in range(gathered.shape[0])
    ]
    bring(own, z, 0, NX)
    for back, src in ((1, f1), (2, f2), (3, f3)):
        bring(src, lax.rem(z + NZ - back, NZ), 0, NX)
    for ahead, src in ((1, b1), (2, b2), (3, b3)):
        bring(src, lax.rem(z + ahead, NZ), 0, NX)
    opposite = lax.rem(z + NZ // 2, NZ)
    bring(f4, opposite, 0, NX // 2)
    bring(b4, opposite, NX // 2, NX // 2)
    for copy in row_copies:
        copy.start()
    for copy in amp_copies:
        copy.wait()
    acc[...] = drive[...]
    for r, copy in enumerate(row_copies):
        copy.wait()
        part = jnp.dot(
            amps_v[r // 2, 2 * (r % 2)], rows_v[r, 0:256, :], preferred_element_type=F32
        )
        part += jnp.dot(
            amps_v[r // 2, 2 * (r % 2) + 1], rows_v[r, 256:512, :], preferred_element_type=F32
        )
        part += jnp.dot(
            hole[:, 256 * r : 256 * (r + 1)], rows_v[r, 512:768, :], preferred_element_type=F32
        )
        acc[...] += part
    residual = acc[...]
    residual_ref[...] = residual
    denominator = pair_energy[...] - own_energy[...]
    updated_ref[...] = (amps[...].astype(F32) - residual / denominator).astype(BF16)


def final(where, gathered, ring, hole, amps, drive, own_energy, pair_energy):
    any_spec = pl.BlockSpec(memory_space=pl.ANY)
    vmem = pl.BlockSpec(memory_space=pltpu.VMEM)
    n = gathered.shape[0]
    return pl.pallas_call(
        final_kernel,
        out_shape=(
            jax.ShapeDtypeStruct(drive.shape, F32),
            jax.ShapeDtypeStruct(amps.shape, BF16),
        ),
        in_specs=[pl.BlockSpec(memory_space=pltpu.SMEM)] + [any_spec] * (1 + len(ring)) + [vmem] * 5,
        out_specs=(vmem, vmem),
        scratch_shapes=[
            pltpu.VMEM(gathered.shape, BF16),
            pltpu.VMEM((NZ, NX) + amps.shape, BF16),
            pltpu.VMEM(drive.shape, F32),
            pltpu.SemaphoreType.DMA((n,)),
            pltpu.SemaphoreType.DMA((NZ + 1,)),
        ],
        compiler_params=pltpu.CompilerParams(vmem_limit_bytes=40 << 20),
        cost_estimate=pl.CostEstimate(
            flops=2 * 256 * 256 * 12288, bytes_accessed=13 << 20, transcendentals=0
        ),
    )(where, gathered, *ring, hole, amps, drive, own_energy, pair_energy)


def body(amplitudes, drive, pair_irrep, occ_irrep, ladder_ints, hole_ints, occ_energy, pair_energy):
    z = lax.axis_index("z")
    x = lax.axis_index("x")
    row_rank = lax.axis_index("y") * NCORE + lax.axis_index("core")
    col_rank = z * NX + x
    where = jnp.stack([z, x]).astype(jnp.int32)
    occ_rows, pair_cols = amplitudes.shape
    ladder_rows = ladder_ints.shape[0]
    own_pairs = lax.dynamic_slice_in_dim(pair_irrep, col_rank * pair_cols, pair_cols)
    ladder_labels = lax.dynamic_slice_in_dim(pair_irrep, row_rank * ladder_rows, ladder_rows)
    own_occ = lax.dynamic_slice_in_dim(occ_irrep, row_rank * occ_rows, occ_rows)
    ladder_kept = jnp.where(
        ladder_labels[:, None] == own_pairs[None, :], ladder_ints, jnp.zeros_like(ladder_ints)
    )
    rows = jnp.concatenate([ladder_kept, amplitudes], axis=0)
    gathered = lax.all_gather(rows, ("y", "core"), axis=0, tiled=False)

    from_ahead = lax.ppermute(amplitudes, "x", shift(NX, -1))
    from_behind = lax.ppermute(amplitudes, "x", shift(NX, 1))
    from_opposite = lax.ppermute(amplitudes, "x", shift(NX, 2))
    own = place(where, (amplitudes, from_ahead, from_opposite, from_behind))
    f1 = lax.ppermute(own, "z", shift(NZ, 1))
    b1 = lax.ppermute(own, "z", shift(NZ, -1))
    f2 = lax.ppermute(f1, "z", shift(NZ, 1))
    b2 = lax.ppermute(b1, "z", shift(NZ, -1))
    f3 = lax.ppermute(f2, "z", shift(NZ, 1))
    b3 = lax.ppermute(b2, "z", shift(NZ, -1))
    f4 = lax.ppermute(f3[: NX // 2], "z", shift(NZ, 1))
    b4 = lax.ppermute(b3[NX // 2 :], "z", shift(NZ, -1))

    hole_kept = jnp.where(
        own_occ[:, None] == occ_irrep[None, :], hole_ints, jnp.zeros_like(hole_ints)
    )
    pair_occ = (occ_energy[:, None] + occ_energy[None, :]).reshape(-1)
    own_energy = lax.dynamic_slice_in_dim(pair_occ, row_rank * occ_rows, occ_rows)
    return final(
        where, gathered, (own, f1, f2, f3, f4, b1, b2, b3, b4), hole_kept, amplitudes, drive,
        own_energy[:, None], pair_energy[None, :],
    )


def solution(mesh):
    fine = Mesh(mesh.devices.reshape(NY, NCORE, NZ, NX), ("y", "core", "z", "x"))
    row, col = ("y", "core"), ("z", "x")
    in_specs = (
        P(row, col),
        P(row, col),
        P(),
        P(),
        P(row, col),
        P(row, None),
        P(),
        P(col),
    )
    out_specs = (P(row, col), P(row, col))
    return jax.shard_map(body, mesh=fine, in_specs=in_specs, out_specs=out_specs, check_vma=False)
```

```python
import jax
import jax.numpy as jnp
from jax import lax
from jax.experimental import pallas as pl
from jax.experimental.pallas import tpu as pltpu
from jax.sharding import Mesh, PartitionSpec as P

NY, NCORE, NZ, NX = 8, 2, 8, 4
BF16, F32 = jnp.bfloat16, jnp.float32
LANES = 128


def shift(n, by):
    return [(i, (i + by) % n) for i in range(n)]


def row_rank():
    return lax.axis_index("y") * NCORE + lax.axis_index("core")


def prep_kernel(labels, ladder, amps, rows_ref):
    r = row_rank()
    c = lax.axis_index("z") * NX + lax.axis_index("x")
    n_ladder, n_cols = ladder.shape
    col_labels = [
        labels[pl.ds(c * (n_cols // LANES) + q, 1), :].astype(F32) for q in range(n_cols // LANES)
    ]
    for k in range(n_ladder // LANES):
        line = labels[pl.ds(r * (n_ladder // LANES) + k, 1), :].astype(F32)
        row_labels = jnp.broadcast_to(line, (LANES, LANES)).T
        for q in range(n_cols // LANES):
            at = (pl.ds(k * LANES, LANES), pl.ds(q * LANES, LANES))
            kept = jnp.where(row_labels == col_labels[q], ladder[at].astype(F32), 0.0)
            rows_ref[at] = kept.astype(BF16)
    rows_ref[n_ladder:, :] = amps[...]


def prep(labels, ladder, amps):
    vmem = pl.BlockSpec(memory_space=pltpu.VMEM)
    n = ladder.shape[0] + amps.shape[0]
    return pl.pallas_call(
        prep_kernel,
        out_shape=jax.ShapeDtypeStruct((n, amps.shape[1]), BF16),
        in_specs=[vmem] * 3,
        out_specs=vmem,
        cost_estimate=pl.CostEstimate(flops=0, bytes_accessed=1 << 20, transcendentals=0),
    )(labels, ladder, amps)


def final_kernel(gathered, hole, *refs):
    parts, (amps, drive, own_energy, pair_energy, residual_ref, updated_ref) = refs[:9], refs[9:15]
    rows_v, amps_rows_v, hole_v, parts_v, acc, row_sems, amps_sems, hole_sems, part_sems = refs[15:]
    z, x = lax.axis_index("z"), lax.axis_index("x")
    n, size = gathered.shape[0], amps.shape[0]
    group = n // len(hole_v)
    hole_copies, copies, at = [], [], 0
    for g in range(len(hole_v)):
        src = hole.at[:, pl.ds(g * group * size, group * size)]
        mine = [pltpu.make_async_copy(src, hole_v[g], hole_sems.at[g])]
        for r in range(g * group, (g + 1) * group):
            src = gathered.at[r, pl.ds(2 * size, size)]
            dst = amps_rows_v.at[pl.ds(r * size, size)]
            mine.append(pltpu.make_async_copy(src, dst, amps_sems.at[r]))
        hole_copies.append(mine)
    opposite = lax.rem(z + NZ // 2, NZ)
    sources = [(lax.rem(z + NZ + away, NZ), range(NX)) for away in (0, -1, 1, -2, 2, -3, 3)]
    sources += [(opposite, range(NX // 2)), (opposite, range(NX // 2, NX))]
    for i, (slot, blocks) in enumerate(sources):
        mine = [pltpu.make_async_copy(parts[i], parts_v[i], part_sems.at[i])]
        for j in blocks:
            block = slot * NX + lax.rem(x + j, NX)
            src = gathered.at[block // 2, pl.ds(pl.multiple_of(lax.rem(block, 2) * size, size), size)]
            dst = rows_v.at[pl.ds(at, size)]
            mine.append(pltpu.make_async_copy(src, dst, row_sems.at[at // size]))
            at += size
        copies.append(mine)
    for mine in hole_copies + copies:
        for copy in mine:
            copy.start()
    acc[...] = drive[...]
    for g, mine in enumerate(hole_copies):
        for copy in mine:
            copy.wait()
        at = pl.ds(g * group * size, group * size)
        acc[...] += jnp.dot(hole_v[g][...], amps_rows_v[at], preferred_element_type=F32)
    at = 0
    for i, mine in enumerate(copies):
        for copy in mine:
            copy.wait()
        depth = size * (len(mine) - 1)
        acc[...] += jnp.dot(parts_v[i][...], rows_v[at : at + depth, :], preferred_element_type=F32)
        at += depth
    residual = acc[...]
    residual_ref[...] = residual
    denominator = pair_energy[...] - own_energy[...]
    updated_ref[...] = (amps[...].astype(F32) - residual / denominator).astype(BF16)


def final(gathered, hole, parts, amps, drive, own_energy, pair_energy):
    hbm = pl.BlockSpec(memory_space=pltpu.HBM)
    vmem = pl.BlockSpec(memory_space=pltpu.VMEM)
    n, _, cols = gathered.shape
    size, groups = amps.shape[0], 4
    in_hbm = [pltpu.with_memory_space_constraint(a, pltpu.HBM) for a in (gathered, hole, *parts)]
    return pl.pallas_call(
        final_kernel,
        out_shape=(
            jax.ShapeDtypeStruct(drive.shape, F32),
            jax.ShapeDtypeStruct(amps.shape, BF16),
        ),
        in_specs=[hbm] * len(in_hbm) + [vmem] * 4,
        out_specs=(vmem, vmem),
        scratch_shapes=[
            pltpu.VMEM((2 * n * size, cols), BF16),
            pltpu.VMEM((n * size, cols), BF16),
            [pltpu.VMEM((size, n * size // groups), BF16) for _ in range(groups)],
            [pltpu.VMEM(p.shape, BF16) for p in parts],
            pltpu.VMEM(drive.shape, F32),
            pltpu.SemaphoreType.DMA((2 * n,)),
            pltpu.SemaphoreType.DMA((n,)),
            pltpu.SemaphoreType.DMA((groups,)),
            pltpu.SemaphoreType.DMA((len(parts),)),
        ],
        compiler_params=pltpu.CompilerParams(vmem_limit_bytes=32 << 20),
        cost_estimate=pl.CostEstimate(
            flops=2 * 256 * 256 * 12288, bytes_accessed=13 << 20, transcendentals=0
        ),
    )(*in_hbm, amps, drive, own_energy, pair_energy)


def body(amplitudes, drive, pair_irrep, occ_irrep, ladder_ints, hole_ints, occ_energy, pair_energy):
    occ_rows = amplitudes.shape[0]
    rows = prep(pair_irrep.reshape(-1, LANES), ladder_ints, amplitudes)
    gathered = lax.all_gather(rows, ("y", "core"), axis=0, tiled=False)

    blocks = [lax.ppermute(amplitudes, "x", shift(NX, -j)) for j in range(1, NX)]
    own = jnp.concatenate([amplitudes] + blocks, axis=1)
    f, b = own, own
    parts = [own]
    for _ in range(NZ // 2 - 1):
        f = lax.ppermute(f, "z", shift(NZ, 1))
        b = lax.ppermute(b, "z", shift(NZ, -1))
        parts += [f, b]
    half = own.shape[1] // 2
    parts.append(lax.ppermute(f[:, :half], "z", shift(NZ, 1)))
    parts.append(lax.ppermute(b[:, half:], "z", shift(NZ, -1)))

    own_occ = lax.dynamic_slice_in_dim(occ_irrep, row_rank() * occ_rows, occ_rows)
    hole_kept = jnp.where(
        own_occ[:, None] == occ_irrep[None, :], hole_ints, jnp.zeros_like(hole_ints)
    )
    pair_occ = (occ_energy[:, None] + occ_energy[None, :]).reshape(-1)
    own_energy = lax.dynamic_slice_in_dim(pair_occ, row_rank() * occ_rows, occ_rows)
    return final(
        gathered, hole_kept, parts, amplitudes, drive, own_energy[:, None], pair_energy[None, :]
    )


def solution(mesh):
    fine = Mesh(mesh.devices.reshape(NY, NCORE, NZ, NX), ("y", "core", "z", "x"))
    row, col = ("y", "core"), ("z", "x")
    in_specs = (
        P(row, col),
        P(row, col),
        P(),
        P(),
        P(row, col),
        P(row, None),
        P(),
        P(col),
    )
    out_specs = (P(row, col), P(row, col))
    return jax.shard_map(body, mesh=fine, in_specs=in_specs, out_specs=out_specs, check_vma=False)
```

```python
import jax
import jax.numpy as jnp
from jax import lax
from jax.experimental import pallas as pl
from jax.experimental.pallas import tpu as pltpu
from jax.sharding import Mesh, PartitionSpec as P

NY, NCORE, NZ, NX = 8, 2, 8, 4
BF16, F32 = jnp.bfloat16, jnp.float32
LANES = 128


def shift(n, by):
    return [(i, (i + by) % n) for i in range(n)]


def row_rank():
    return lax.axis_index("y") * NCORE + lax.axis_index("core")


def kept_block():
    x = lax.axis_index("x")
    inner = jnp.logical_or(x == 1, x == 2).astype(jnp.int32)
    return lax.rem(inner + lax.axis_index("core"), 2)


def masked_block(labels, ladder, block, write):
    r = row_rank()
    c = lax.axis_index("z") * NX + lax.axis_index("x")
    size = ladder.shape[0] // 2
    lines, cols = size // LANES, ladder.shape[1] // LANES
    col_labels = [labels[pl.ds(c * cols + q, 1), :].astype(F32) for q in range(cols)]
    for k in range(lines):
        line = labels[pl.ds((2 * r + block) * lines + k, 1), :].astype(F32)
        row_labels = jnp.broadcast_to(line, (LANES, LANES)).T
        at = pl.ds(pl.multiple_of(block * size + k * LANES, LANES), LANES)
        for q in range(cols):
            lanes = slice(q * LANES, (q + 1) * LANES)
            values = ladder[at, lanes].astype(F32)
            kept = jnp.where(row_labels == col_labels[q], values, 0.0)
            write(slice(k * LANES, (k + 1) * LANES), lanes, kept.astype(BF16))


def send_kernel(labels, ladder, out_ref):
    def write(rows, lanes, values):
        out_ref[rows, lanes] = values

    masked_block(labels, ladder, 1 - kept_block(), write)


def rows_kernel(labels, ladder, amps, out_ref):
    def write(rows, lanes, values):
        out_ref[rows, lanes] = values

    masked_block(labels, ladder, kept_block(), write)
    size = amps.shape[0]
    out_ref[size : 2 * size, :] = amps[...]
    out_ref[2 * size :, :] = jnp.zeros_like(amps)


def prepare(kernel, rows, *args):
    vmem = pl.BlockSpec(memory_space=pltpu.VMEM)
    return pl.pallas_call(
        kernel,
        out_shape=jax.ShapeDtypeStruct((rows, args[1].shape[1]), BF16),
        in_specs=[vmem] * len(args),
        out_specs=vmem,
        cost_estimate=pl.CostEstimate(flops=0, bytes_accessed=1 << 20, transcendentals=0),
    )(*args)


def ladder_copies(gathered, first_row, parts, parts_v, part_sems, rows_v, row_sems, size):
    z, x = lax.axis_index("z"), lax.axis_index("x")
    upper = (x >= NX // 2).astype(jnp.int32)
    opposite = lax.rem(z + NZ // 2, NZ)
    sources = [(lax.rem(z + NZ + away, NZ), (0, 1)) for away in (0, -1, 1, -2, 2, -3, 3)]
    sources += [(opposite, (0,)), (opposite, (1,))]
    copies, at = [], 0
    for i, (slot, blocks) in enumerate(sources):
        mine = [pltpu.make_async_copy(parts[i], parts_v[i], part_sems.at[i])]
        for j in blocks:
            r = 2 * slot + (upper if j == 0 else 1 - upper)
            src = gathered.at[r, pl.ds(first_row, size)]
            dst = rows_v.at[pl.ds(at, size)]
            mine.append(pltpu.make_async_copy(src, dst, row_sems.at[at // size]))
            at += size
        copies.append(mine)
    return copies


def add_ladder(copies, parts_v, rows_v, acc, size):
    at = 0
    for i, mine in enumerate(copies):
        for copy in mine:
            copy.wait()
        depth = size * (len(mine) - 1)
        acc[...] += jnp.dot(parts_v[i][...], rows_v[at : at + depth, :], preferred_element_type=F32)
        at += depth


def partner_kernel(gathered, *refs):
    parts, out_ref = refs[:9], refs[9]
    rows_v, parts_v, row_sems, part_sems = refs[10:]
    size = out_ref.shape[0]
    copies = ladder_copies(gathered, 2 * size, parts, parts_v, part_sems, rows_v, row_sems, size)
    for mine in copies:
        for copy in mine:
            copy.start()
    out_ref[...] = jnp.zeros_like(out_ref)
    add_ladder(copies, parts_v, rows_v, out_ref, size)


def own_kernel(gathered, hole, *refs):
    parts, drive, out_ref = refs[:9], refs[9], refs[10]
    rows_v, amps_rows_v, hole_v, parts_v, row_sems, amps_sems, hole_sems, part_sems = refs[11:]
    n, size = gathered.shape[0], out_ref.shape[0]
    group = n // len(hole_v)
    hole_copies = []
    for g in range(len(hole_v)):
        src = hole.at[:, pl.ds(g * group * size, group * size)]
        mine = [pltpu.make_async_copy(src, hole_v[g], hole_sems.at[g])]
        for r in range(g * group, (g + 1) * group):
            src = gathered.at[r, pl.ds(size, size)]
            dst = amps_rows_v.at[pl.ds(r * size, size)]
            mine.append(pltpu.make_async_copy(src, dst, amps_sems.at[r]))
        hole_copies.append(mine)
    copies = ladder_copies(gathered, 0, parts, parts_v, part_sems, rows_v, row_sems, size)
    for mine in hole_copies + copies:
        for copy in mine:
            copy.start()
    out_ref[...] = drive[...]
    for g, mine in enumerate(hole_copies):
        for copy in mine:
            copy.wait()
        at = pl.ds(g * group * size, group * size)
        out_ref[...] += jnp.dot(hole_v[g][...], amps_rows_v[at], preferred_element_type=F32)
    add_ladder(copies, parts_v, rows_v, out_ref, size)


def products(kernel, gathered, hole, parts, drive):
    hbm = pl.BlockSpec(memory_space=pltpu.HBM)
    vmem = pl.BlockSpec(memory_space=pltpu.VMEM)
    n, _, cols = gathered.shape
    size, groups = drive.shape[0], 4
    with_hole = hole is not None
    arrays = (gathered, hole, *parts) if with_hole else (gathered, *parts)
    in_hbm = [pltpu.with_memory_space_constraint(a, pltpu.HBM) for a in arrays]
    scratch = [pltpu.VMEM((n * size, cols), BF16)]
    sems = [pltpu.SemaphoreType.DMA((n,))]
    if with_hole:
        scratch.append(pltpu.VMEM((n * size, cols), BF16))
        scratch.append([pltpu.VMEM((size, n * size // groups), BF16) for _ in range(groups)])
        sems += [pltpu.SemaphoreType.DMA((n,)), pltpu.SemaphoreType.DMA((groups,))]
    scratch.append([pltpu.VMEM(p.shape, BF16) for p in parts])
    sems.append(pltpu.SemaphoreType.DMA((len(parts),)))
    depth = (2 if with_hole else 1) * n * size
    return pl.pallas_call(
        kernel,
        out_shape=jax.ShapeDtypeStruct(drive.shape, F32),
        in_specs=[hbm] * len(in_hbm) + ([vmem] if with_hole else []),
        out_specs=vmem,
        scratch_shapes=scratch + sems,
        compiler_params=pltpu.CompilerParams(vmem_limit_bytes=32 << 20),
        cost_estimate=pl.CostEstimate(
            flops=2 * size * cols * depth, bytes_accessed=4 * size * depth, transcendentals=0
        ),
    )(*in_hbm, *([drive] if with_hole else []))


def body(amplitudes, drive, pair_irrep, occ_irrep, ladder_ints, hole_ints, occ_energy, pair_energy):
    size = amplitudes.shape[0]
    labels = pair_irrep.reshape(-1, LANES)
    partner = [(i, i ^ 1) for i in range(NX)]
    lent = lax.ppermute(prepare(send_kernel, size, labels, ladder_ints), "x", partner)
    rows = prepare(rows_kernel, 3 * size, labels, ladder_ints, amplitudes)
    rows = lax.dynamic_update_slice(rows, lent, (2 * size, 0))
    gathered = lax.all_gather(rows, ("y", "core"), axis=0, tiled=False)

    other = lax.ppermute(amplitudes, "x", [(i, NX - 1 - i) for i in range(NX)])
    own = jnp.concatenate([amplitudes, other], axis=1)
    f, b = own, own
    parts = [own]
    for _ in range(NZ // 2 - 1):
        f = lax.ppermute(f, "z", shift(NZ, 1))
        b = lax.ppermute(b, "z", shift(NZ, -1))
        parts += [f, b]
    parts.append(lax.ppermute(f[:, :size], "z", shift(NZ, 1)))
    parts.append(lax.ppermute(b[:, size:], "z", shift(NZ, -1)))

    own_occ = lax.dynamic_slice_in_dim(occ_irrep, row_rank() * size, size)
    hole_kept = jnp.where(
        own_occ[:, None] == occ_irrep[None, :], hole_ints, jnp.zeros_like(hole_ints)
    )
    pair_occ = (occ_energy[:, None] + occ_energy[None, :]).reshape(-1)
    own_energy = lax.dynamic_slice_in_dim(pair_occ, row_rank() * size, size)
    denominator = pair_energy[None, :] - own_energy[:, None]
    for_partner = products(partner_kernel, gathered, None, parts, drive)
    from_partner = lax.ppermute(for_partner, "x", partner)
    residual = products(own_kernel, gathered, hole_kept, parts, drive) + from_partner
    updated = (amplitudes.astype(F32) - residual / denominator).astype(BF16)
    return residual, updated


def solution(mesh):
    fine = Mesh(mesh.devices.reshape(NY, NCORE, NZ, NX), ("y", "core", "z", "x"))
    row, col = ("y", "core"), ("z", "x")
    in_specs = (
        P(row, col),
        P(row, col),
        P(),
        P(),
        P(row, col),
        P(row, None),
        P(),
        P(col),
    )
    out_specs = (P(row, col), P(row, col))
    return jax.shard_map(body, mesh=fine, in_specs=in_specs, out_specs=out_specs, check_vma=False)
```

```python
import jax
import jax.numpy as jnp
from jax import lax
from jax.experimental import pallas as pl
from jax.experimental.pallas import tpu as pltpu
from jax.sharding import Mesh, PartitionSpec as P

NY, NCORE, NZ, NX = 8, 2, 8, 4
BF16, F32 = jnp.bfloat16, jnp.float32
LANES = 128
FIXED_BITS = 14
EXPONENT_ROWS = 16


def shift(n, by):
    return [(i, (i + by) % n) for i in range(n)]


def row_rank():
    return lax.axis_index("y") * NCORE + lax.axis_index("core")


def kept_block():
    x = lax.axis_index("x")
    inner = jnp.logical_or(x == 1, x == 2).astype(jnp.int32)
    return lax.rem(inner + lax.axis_index("core"), 2)


def masked_block(labels, ladder, block, write):
    r = row_rank()
    c = lax.axis_index("z") * NX + lax.axis_index("x")
    size = ladder.shape[0] // 2
    lines, cols = size // LANES, ladder.shape[1] // LANES
    col_labels = [labels[pl.ds(c * cols + q, 1), :].astype(F32) for q in range(cols)]
    for k in range(lines):
        line = labels[pl.ds((2 * r + block) * lines + k, 1), :].astype(F32)
        row_labels = jnp.broadcast_to(line, (LANES, LANES)).T
        at = pl.ds(pl.multiple_of(block * size + k * LANES, LANES), LANES)
        for q in range(cols):
            lanes = slice(q * LANES, (q + 1) * LANES)
            values = ladder[at, lanes].astype(F32)
            kept = jnp.where(row_labels == col_labels[q], values, 0.0)
            write(slice(k * LANES, (k + 1) * LANES), lanes, kept.astype(BF16))


def send_kernel(labels, ladder, out_ref):
    def write(rows, lanes, values):
        out_ref[rows, lanes] = values

    masked_block(labels, ladder, 1 - kept_block(), write)


def rows_kernel(labels, ladder, amps, out_ref):
    def write(rows, lanes, values):
        out_ref[rows, lanes] = values

    masked_block(labels, ladder, kept_block(), write)
    size = amps.shape[0]
    out_ref[size : 2 * size, :] = amps[...]
    out_ref[2 * size :, :] = jnp.zeros_like(amps)


def prepare(kernel, rows, *args):
    vmem = pl.BlockSpec(memory_space=pltpu.VMEM)
    return pl.pallas_call(
        kernel,
        out_shape=jax.ShapeDtypeStruct((rows, args[1].shape[1]), BF16),
        in_specs=[vmem] * len(args),
        out_specs=vmem,
        cost_estimate=pl.CostEstimate(flops=0, bytes_accessed=1 << 20, transcendentals=0),
    )(*args)


def ladder_copies(gathered, first_row, parts, rows_v, row_sems, size):
    z, x = lax.axis_index("z"), lax.axis_index("x")
    upper = (x >= NX // 2).astype(jnp.int32)
    opposite = lax.rem(z + NZ // 2, NZ)
    sources = [(lax.rem(z + NZ + away, NZ), (0, 1)) for away in (0, -1, 1, -2, 2, -3, 3)]
    sources += [(opposite, (0,)), (opposite, (1,))]
    copies, at = [], 0
    for slot, blocks in sources:
        mine = []
        for j in blocks:
            r = 2 * slot + (upper if j == 0 else 1 - upper)
            src = gathered.at[r, pl.ds(first_row, size)]
            dst = rows_v.at[pl.ds(at, size)]
            mine.append(pltpu.make_async_copy(src, dst, row_sems.at[at // size]))
            at += size
        copies.append(mine)
    return copies


def add_ladder(copies, parts, rows_v, acc, size):
    at = 0
    for part, mine in zip(parts, copies):
        for copy in mine:
            copy.wait()
        depth = size * len(mine)
        acc[...] += jnp.dot(part[...], rows_v[at : at + depth, :], preferred_element_type=F32)
        at += depth


def partner_kernel(gathered, *refs):
    parts, out_ref, rows_v, acc, row_sems = refs[:9], *refs[9:]
    size = acc.shape[0]
    copies = ladder_copies(gathered, 2 * size, parts, rows_v, row_sems, size)
    for mine in copies:
        for copy in mine:
            copy.start()
    acc[...] = jnp.zeros_like(acc)
    add_ladder(copies, parts, rows_v, acc, size)
    largest = jnp.max(jnp.abs(acc[...]), axis=0, keepdims=True)
    exponent = jnp.ceil(jnp.log2(jnp.maximum(largest, 2.0**-100)))
    fixed = jnp.round(acc[...] * jnp.exp2(FIXED_BITS - exponent))
    out_ref[:size, :] = fixed.astype(jnp.int32).astype(jnp.int16)
    rows = out_ref.shape[0] - size
    line = jnp.broadcast_to(exponent, (rows, exponent.shape[1]))
    out_ref[size:, :] = line.astype(jnp.int32).astype(jnp.int16)


def own_kernel(gathered, hole, *refs):
    parts, drive, out_ref = refs[:9], refs[9], refs[10]
    rows_v, amps_rows_v, hole_v, row_sems, amps_sems, hole_sems = refs[11:]
    n, size = gathered.shape[0], out_ref.shape[0]
    group = n // len(hole_v)
    hole_copies = []
    for g in range(len(hole_v)):
        src = hole.at[:, pl.ds(g * group * size, group * size)]
        mine = [pltpu.make_async_copy(src, hole_v[g], hole_sems.at[g])]
        for r in range(g * group, (g + 1) * group):
            src = gathered.at[r, pl.ds(size, size)]
            dst = amps_rows_v.at[pl.ds(r * size, size)]
            mine.append(pltpu.make_async_copy(src, dst, amps_sems.at[r]))
        hole_copies.append(mine)
    copies = ladder_copies(gathered, 0, parts, rows_v, row_sems, size)
    for mine in copies + hole_copies:
        for copy in mine:
            copy.start()
    out_ref[...] = drive[...]
    add_ladder(copies, parts, rows_v, out_ref, size)
    for g, mine in enumerate(hole_copies):
        for copy in mine:
            copy.wait()
        at = pl.ds(g * group * size, group * size)
        out_ref[...] += jnp.dot(hole_v[g][...], amps_rows_v[at], preferred_element_type=F32)


def products(kernel, gathered, hole, parts, drive):
    hbm = pl.BlockSpec(memory_space=pltpu.HBM)
    vmem = pl.BlockSpec(memory_space=pltpu.VMEM)
    n, _, cols = gathered.shape
    size, groups = drive.shape[0], 4
    with_hole = hole is not None
    arrays = (gathered, hole) if with_hole else (gathered,)
    in_hbm = [pltpu.with_memory_space_constraint(a, pltpu.HBM) for a in arrays]
    in_vmem = (*parts, drive) if with_hole else parts
    out = jax.ShapeDtypeStruct(drive.shape, F32)
    scratch = [pltpu.VMEM((n * size, cols), BF16)]
    if not with_hole:
        out = jax.ShapeDtypeStruct((size + EXPONENT_ROWS, cols), jnp.int16)
        scratch.append(pltpu.VMEM(drive.shape, F32))
    sems = [pltpu.SemaphoreType.DMA((n,))]
    if with_hole:
        scratch.append(pltpu.VMEM((n * size, cols), BF16))
        scratch.append([pltpu.VMEM((size, n * size // groups), BF16) for _ in range(groups)])
        sems += [pltpu.SemaphoreType.DMA((n,)), pltpu.SemaphoreType.DMA((groups,))]
    depth = (2 if with_hole else 1) * n * size
    return pl.pallas_call(
        kernel,
        out_shape=out,
        in_specs=[hbm] * len(in_hbm) + [vmem] * len(in_vmem),
        out_specs=vmem,
        scratch_shapes=scratch + sems,
        compiler_params=pltpu.CompilerParams(vmem_limit_bytes=24 << 20),
        cost_estimate=pl.CostEstimate(
            flops=2 * size * cols * depth, bytes_accessed=4 * size * depth, transcendentals=0
        ),
    )(*in_hbm, *in_vmem)


def body(amplitudes, drive, pair_irrep, occ_irrep, ladder_ints, hole_ints, occ_energy, pair_energy):
    size = amplitudes.shape[0]
    labels = pair_irrep.reshape(-1, LANES)
    partner = [(i, i ^ 1) for i in range(NX)]
    lent = lax.ppermute(prepare(send_kernel, size, labels, ladder_ints), "x", partner)
    rows = prepare(rows_kernel, 3 * size, labels, ladder_ints, amplitudes)
    rows = lax.dynamic_update_slice(rows, lent, (2 * size, 0))
    gathered = lax.all_gather(rows, ("y", "core"), axis=0, tiled=False)

    other = lax.ppermute(amplitudes, "x", [(i, NX - 1 - i) for i in range(NX)])
    own = jnp.concatenate([amplitudes, other], axis=1)
    f, b = own, own
    parts = [own]
    for _ in range(NZ // 2 - 1):
        f = lax.ppermute(f, "z", shift(NZ, 1))
        b = lax.ppermute(b, "z", shift(NZ, -1))
        parts += [f, b]
    parts.append(lax.ppermute(f[:, :size], "z", shift(NZ, 1)))
    parts.append(lax.ppermute(b[:, size:], "z", shift(NZ, -1)))

    own_occ = lax.dynamic_slice_in_dim(occ_irrep, row_rank() * size, size)
    hole_kept = jnp.where(
        own_occ[:, None] == occ_irrep[None, :], hole_ints, jnp.zeros_like(hole_ints)
    )
    pair_occ = (occ_energy[:, None] + occ_energy[None, :]).reshape(-1)
    own_energy = lax.dynamic_slice_in_dim(pair_occ, row_rank() * size, size)
    denominator = pair_energy[None, :] - own_energy[:, None]
    for_partner = products(partner_kernel, gathered, None, parts, drive)
    from_partner = lax.ppermute(for_partner, "x", partner)
    scale = jnp.exp2(from_partner[size : size + 1].astype(F32) - FIXED_BITS)
    residual = products(own_kernel, gathered, hole_kept, parts, drive)
    residual = residual + from_partner[:size].astype(F32) * scale
    updated = (amplitudes.astype(F32) - residual / denominator).astype(BF16)
    return residual, updated


def solution(mesh):
    fine = Mesh(mesh.devices.reshape(NY, NCORE, NZ, NX), ("y", "core", "z", "x"))
    row, col = ("y", "core"), ("z", "x")
    in_specs = (
        P(row, col),
        P(row, col),
        P(),
        P(),
        P(row, col),
        P(row, None),
        P(),
        P(col),
    )
    out_specs = (P(row, col), P(row, col))
    return jax.shard_map(body, mesh=fine, in_specs=in_specs, out_specs=out_specs, check_vma=False)
```

```python
import jax
import jax.numpy as jnp
from jax import lax
from jax.experimental import pallas as pl
from jax.experimental.pallas import tpu as pltpu
from jax.sharding import Mesh, PartitionSpec as P

NY, NCORE, NZ, NX = 8, 2, 8, 4
BF16, F32 = jnp.bfloat16, jnp.float32
LANES = 128
FIXED_BITS = 14
EXPONENT_ROWS = 16


def shift(n, by):
    return [(i, (i + by) % n) for i in range(n)]


def row_rank():
    return lax.axis_index("y") * NCORE + lax.axis_index("core")


def kept_block():
    x = lax.axis_index("x")
    inner = jnp.logical_or(x == 1, x == 2).astype(jnp.int32)
    return lax.rem(inner + lax.axis_index("core"), 2)


def masked(values, row_labels, col_labels):
    return jnp.where(row_labels == col_labels, values.astype(F32), 0.0).astype(BF16)


def down(line):
    return jnp.broadcast_to(line.astype(F32), (LANES, LANES)).T


def rows_kernel(labels, ladder, amps, out_ref):
    size, cols = amps.shape
    block = kept_block()
    c = lax.axis_index("z") * NX + lax.axis_index("x")
    lines = cols // LANES
    first = (2 * row_rank() + block) * (size // LANES)
    for k in range(size // LANES):
        row_labels = down(labels[pl.ds(first + k, 1), :])
        at = pl.ds(pl.multiple_of(block * size + k * LANES, LANES), LANES)
        for q in range(lines):
            lanes = slice(q * LANES, (q + 1) * LANES)
            col_labels = labels[pl.ds(c * lines + q, 1), :].astype(F32)
            out_ref[k * LANES : (k + 1) * LANES, lanes] = masked(ladder[at, lanes], row_labels, col_labels)
    out_ref[size : 2 * size, :] = amps[...]
    out_ref[2 * size :, :] = jnp.zeros_like(amps)


def gather_rows(labels, ladder, amps):
    vmem = pl.BlockSpec(memory_space=pltpu.VMEM)
    size, cols = amps.shape
    return pl.pallas_call(
        rows_kernel,
        out_shape=jax.ShapeDtypeStruct((3 * size, cols), BF16),
        in_specs=[vmem] * 3,
        out_specs=vmem,
        cost_estimate=pl.CostEstimate(flops=0, bytes_accessed=1 << 20, transcendentals=0),
    )(labels, ladder, amps)


def ladder_copies(gathered, first_row, parts, rows_v, row_sems, size):
    z, x = lax.axis_index("z"), lax.axis_index("x")
    upper = (x >= NX // 2).astype(jnp.int32)
    opposite = lax.rem(z + NZ // 2, NZ)
    sources = [(lax.rem(z + NZ + away, NZ), (0, 1)) for away in (0, -1, 1, -2, 2, -3, 3)]
    sources += [(opposite, (0,)), (opposite, (1,))]
    copies, at = [], 0
    for slot, blocks in sources:
        mine = []
        for j in blocks:
            r = 2 * slot + (upper if j == 0 else 1 - upper)
            src = gathered.at[r, pl.ds(first_row, size)]
            dst = rows_v.at[pl.ds(at, size)]
            mine.append(pltpu.make_async_copy(src, dst, row_sems.at[at // size]))
            at += size
        copies.append(mine)
    return copies


def add_ladder(copies, parts, rows_v, acc, size):
    at = 0
    for part, mine in zip(parts, copies):
        for copy in mine:
            copy.wait()
        depth = size * len(mine)
        acc[...] += jnp.dot(part[...], rows_v[at : at + depth, :], preferred_element_type=F32)
        at += depth


def partner_kernel(gathered, *refs):
    parts, out_ref, rows_v, acc, row_sems = refs[:9], *refs[9:]
    size = acc.shape[0]
    copies = ladder_copies(gathered, 2 * size, parts, rows_v, row_sems, size)
    for mine in copies:
        for copy in mine:
            copy.start()
    acc[...] = jnp.zeros_like(acc)
    add_ladder(copies, parts, rows_v, acc, size)
    largest = jnp.max(jnp.abs(acc[...]), axis=0, keepdims=True)
    exponent = jnp.ceil(jnp.log2(jnp.maximum(largest, 2.0**-100)))
    fixed = jnp.round(acc[...] * jnp.exp2(FIXED_BITS - exponent))
    out_ref[:size, :] = fixed.astype(jnp.int32).astype(jnp.int16)
    rows = out_ref.shape[0] - size
    line = jnp.broadcast_to(exponent, (rows, exponent.shape[1]))
    out_ref[size:, :] = line.astype(jnp.int32).astype(jnp.int16)


def own_kernel(gathered, hole, *refs):
    parts, drive, out_ref = refs[:9], refs[9], refs[10]
    rows_v, amps_rows_v, hole_v, row_sems, amps_sems, hole_sems = refs[11:]
    n, size = gathered.shape[0], out_ref.shape[0]
    group = n // len(hole_v)
    hole_copies = []
    for g in range(len(hole_v)):
        src = hole.at[:, pl.ds(g * group * size, group * size)]
        mine = [pltpu.make_async_copy(src, hole_v[g], hole_sems.at[g])]
        for r in range(g * group, (g + 1) * group):
            src = gathered.at[r, pl.ds(size, size)]
            dst = amps_rows_v.at[pl.ds(r * size, size)]
            mine.append(pltpu.make_async_copy(src, dst, amps_sems.at[r]))
        hole_copies.append(mine)
    copies = ladder_copies(gathered, 0, parts, rows_v, row_sems, size)
    for mine in copies + hole_copies:
        for copy in mine:
            copy.start()
    out_ref[...] = drive[...]
    add_ladder(copies, parts, rows_v, out_ref, size)
    for g, mine in enumerate(hole_copies):
        for copy in mine:
            copy.wait()
        at = pl.ds(g * group * size, group * size)
        out_ref[...] += jnp.dot(hole_v[g][...], amps_rows_v[at], preferred_element_type=F32)


def products(kernel, gathered, hole, parts, drive):
    hbm = pl.BlockSpec(memory_space=pltpu.HBM)
    vmem = pl.BlockSpec(memory_space=pltpu.VMEM)
    n, _, cols = gathered.shape
    size, groups = drive.shape[0], 4
    with_hole = hole is not None
    arrays = (gathered, hole) if with_hole else (gathered,)
    in_hbm = [pltpu.with_memory_space_constraint(a, pltpu.HBM) for a in arrays]
    in_vmem = (*parts, drive) if with_hole else parts
    out = jax.ShapeDtypeStruct(drive.shape, F32)
    scratch = [pltpu.VMEM((n * size, cols), BF16)]
    if not with_hole:
        out = jax.ShapeDtypeStruct((size + EXPONENT_ROWS, cols), jnp.int16)
        scratch.append(pltpu.VMEM(drive.shape, F32))
    sems = [pltpu.SemaphoreType.DMA((n,))]
    if with_hole:
        scratch.append(pltpu.VMEM((n * size, cols), BF16))
        scratch.append([pltpu.VMEM((size, n * size // groups), BF16) for _ in range(groups)])
        sems += [pltpu.SemaphoreType.DMA((n,)), pltpu.SemaphoreType.DMA((groups,))]
    depth = (2 if with_hole else 1) * n * size
    return pl.pallas_call(
        kernel,
        out_shape=out,
        in_specs=[hbm] * len(in_hbm) + [vmem] * len(in_vmem),
        out_specs=vmem,
        scratch_shapes=scratch + sems,
        compiler_params=pltpu.CompilerParams(vmem_limit_bytes=24 << 20),
        cost_estimate=pl.CostEstimate(
            flops=2 * size * cols * depth, bytes_accessed=4 * size * depth, transcendentals=0
        ),
    )(*in_hbm, *in_vmem)


def body(amplitudes, drive, pair_irrep, occ_irrep, ladder_ints, hole_ints, occ_energy, pair_energy):
    size = amplitudes.shape[0]
    labels = pair_irrep.reshape(-1, LANES)
    partner = [(i, i ^ 1) for i in range(NX)]
    kept = kept_block()
    lent = lax.dynamic_slice_in_dim(ladder_ints, (1 - kept) * size, size)
    lent = lax.ppermute(lent, "x", partner)
    rows = gather_rows(labels, ladder_ints, amplitudes)
    lent_rows = lax.dynamic_slice_in_dim(pair_irrep, (2 * row_rank() + kept) * size, size)
    partner_rank = lax.axis_index("z") * NX + (lax.axis_index("x") ^ 1)
    lent_cols = lax.dynamic_slice_in_dim(pair_irrep, partner_rank * size, size)
    lent = jnp.where(lent_rows[:, None] == lent_cols[None, :], lent, jnp.zeros_like(lent))
    rows = lax.dynamic_update_slice(rows, lent, (2 * size, 0))
    gathered = lax.all_gather(rows, ("y", "core"), axis=0, tiled=False)

    other = lax.ppermute(amplitudes, "x", [(i, NX - 1 - i) for i in range(NX)])
    own = jnp.concatenate([amplitudes, other], axis=1)
    f, b = own, own
    parts = [own]
    for _ in range(NZ // 2 - 1):
        f = lax.ppermute(f, "z", shift(NZ, 1))
        b = lax.ppermute(b, "z", shift(NZ, -1))
        parts += [f, b]
    parts.append(lax.ppermute(f[:, :size], "z", shift(NZ, 1)))
    parts.append(lax.ppermute(b[:, size:], "z", shift(NZ, -1)))

    own_occ = lax.dynamic_slice_in_dim(occ_irrep, row_rank() * size, size)
    hole_kept = jnp.where(
        own_occ[:, None] == occ_irrep[None, :], hole_ints, jnp.zeros_like(hole_ints)
    )
    pair_occ = (occ_energy[:, None] + occ_energy[None, :]).reshape(-1)
    own_energy = lax.dynamic_slice_in_dim(pair_occ, row_rank() * size, size)
    denominator = pair_energy[None, :] - own_energy[:, None]
    for_partner = products(partner_kernel, gathered, None, parts, drive)
    from_partner = lax.ppermute(for_partner, "x", partner)
    scale = jnp.exp2(from_partner[size : size + 1].astype(F32) - FIXED_BITS)
    residual = products(own_kernel, gathered, hole_kept, parts, drive)
    residual = residual + from_partner[:size].astype(F32) * scale
    updated = (amplitudes.astype(F32) - residual / denominator).astype(BF16)
    return residual, updated


def solution(mesh):
    fine = Mesh(mesh.devices.reshape(NY, NCORE, NZ, NX), ("y", "core", "z", "x"))
    row, col = ("y", "core"), ("z", "x")
    in_specs = (
        P(row, col),
        P(row, col),
        P(),
        P(),
        P(row, col),
        P(row, None),
        P(),
        P(col),
    )
    out_specs = (P(row, col), P(row, col))
    return jax.shard_map(body, mesh=fine, in_specs=in_specs, out_specs=out_specs, check_vma=False)
```

```python
import jax
import jax.numpy as jnp
from jax import lax
from jax.experimental import pallas as pl
from jax.experimental.pallas import tpu as pltpu
from jax.sharding import Mesh, PartitionSpec as P

NY, NCORE, NZ, NX = 8, 2, 8, 4
BF16, F32 = jnp.bfloat16, jnp.float32
LANES = 128
FIXED_BITS = 15
FIXED_MOST = 2.0**15 - 1
EXPONENT_ROWS = 16


def shift(n, by):
    return [(i, (i + by) % n) for i in range(n)]


def row_rank():
    return lax.axis_index("y") * NCORE + lax.axis_index("core")


def kept_block():
    x = lax.axis_index("x")
    inner = jnp.logical_or(x == 1, x == 2).astype(jnp.int32)
    return lax.rem(inner + lax.axis_index("core"), 2)


def masked(values, row_labels, col_labels):
    return jnp.where(row_labels == col_labels, values.astype(F32), 0.0).astype(BF16)


def down(line):
    return jnp.broadcast_to(line.astype(F32), (LANES, LANES)).T


def rows_kernel(labels, ladder, amps, out_ref):
    size, cols = amps.shape
    block = kept_block()
    c = lax.axis_index("z") * NX + lax.axis_index("x")
    lines = cols // LANES
    first = (2 * row_rank() + block) * (size // LANES)
    for k in range(size // LANES):
        row_labels = down(labels[pl.ds(first + k, 1), :])
        at = pl.ds(pl.multiple_of(block * size + k * LANES, LANES), LANES)
        for q in range(lines):
            lanes = slice(q * LANES, (q + 1) * LANES)
            col_labels = labels[pl.ds(c * lines + q, 1), :].astype(F32)
            out_ref[k * LANES : (k + 1) * LANES, lanes] = masked(ladder[at, lanes], row_labels, col_labels)
    out_ref[size : 2 * size, :] = amps[...]
    out_ref[2 * size :, :] = jnp.zeros_like(amps)


def gather_rows(labels, ladder, amps):
    vmem = pl.BlockSpec(memory_space=pltpu.VMEM)
    size, cols = amps.shape
    return pl.pallas_call(
        rows_kernel,
        out_shape=jax.ShapeDtypeStruct((3 * size, cols), BF16),
        in_specs=[vmem] * 3,
        out_specs=vmem,
        cost_estimate=pl.CostEstimate(flops=0, bytes_accessed=1 << 20, transcendentals=0),
    )(labels, ladder, amps)


def ladder_copies(gathered, first_row, parts, rows_v, row_sems, size):
    z, x = lax.axis_index("z"), lax.axis_index("x")
    upper = (x >= NX // 2).astype(jnp.int32)
    opposite = lax.rem(z + NZ // 2, NZ)
    sources = [(lax.rem(z + NZ + away, NZ), (0, 1)) for away in (0, -1, 1, -2, 2, -3, 3)]
    sources += [(opposite, (0,)), (opposite, (1,))]
    copies, at = [], 0
    for slot, blocks in sources:
        mine = []
        for j in blocks:
            r = 2 * slot + (upper if j == 0 else 1 - upper)
            src = gathered.at[r, pl.ds(first_row, size)]
            dst = rows_v.at[pl.ds(at, size)]
            mine.append(pltpu.make_async_copy(src, dst, row_sems.at[at // size]))
            at += size
        copies.append(mine)
    return copies


def add_ladder(copies, parts, rows_v, acc, size):
    at = 0
    for part, mine in zip(parts, copies):
        for copy in mine:
            copy.wait()
        depth = size * len(mine)
        acc[...] += jnp.dot(part[...], rows_v[at : at + depth, :], preferred_element_type=F32)
        at += depth


def partner_kernel(gathered, *refs):
    parts, out_ref, rows_v, acc, row_sems = refs[:9], *refs[9:]
    size = acc.shape[0]
    copies = ladder_copies(gathered, 2 * size, parts, rows_v, row_sems, size)
    for mine in copies:
        for copy in mine:
            copy.start()
    acc[...] = jnp.zeros_like(acc)
    add_ladder(copies, parts, rows_v, acc, size)
    largest = jnp.max(jnp.abs(acc[...]), axis=0, keepdims=True)
    exponent = jnp.ceil(jnp.log2(jnp.maximum(largest, 2.0**-100)))
    fixed = jnp.round(acc[...] * jnp.exp2(FIXED_BITS - exponent))
    fixed = jnp.clip(fixed, -FIXED_MOST, FIXED_MOST)
    out_ref[:size, :] = fixed.astype(jnp.int32).astype(jnp.int16)
    rows = out_ref.shape[0] - size
    line = jnp.broadcast_to(exponent, (rows, exponent.shape[1]))
    out_ref[size:, :] = line.astype(jnp.int32).astype(jnp.int16)


def own_kernel(gathered, hole, *refs):
    parts, drive, out_ref = refs[:9], refs[9], refs[10]
    rows_v, amps_rows_v, hole_v, row_sems, amps_sems, hole_sems = refs[11:]
    n, size = gathered.shape[0], out_ref.shape[0]
    group = n // len(hole_v)
    hole_copies = []
    for g in range(len(hole_v)):
        src = hole.at[:, pl.ds(g * group * size, group * size)]
        mine = [pltpu.make_async_copy(src, hole_v[g], hole_sems.at[g])]
        for r in range(g * group, (g + 1) * group):
            src = gathered.at[r, pl.ds(size, size)]
            dst = amps_rows_v.at[pl.ds(r * size, size)]
            mine.append(pltpu.make_async_copy(src, dst, amps_sems.at[r]))
        hole_copies.append(mine)
    copies = ladder_copies(gathered, 0, parts, rows_v, row_sems, size)
    for mine in copies + hole_copies:
        for copy in mine:
            copy.start()
    out_ref[...] = drive[...]
    add_ladder(copies, parts, rows_v, out_ref, size)
    for g, mine in enumerate(hole_copies):
        for copy in mine:
            copy.wait()
        at = pl.ds(g * group * size, group * size)
        out_ref[...] += jnp.dot(hole_v[g][...], amps_rows_v[at], preferred_element_type=F32)


def products(kernel, gathered, hole, parts, drive):
    hbm = pl.BlockSpec(memory_space=pltpu.HBM)
    vmem = pl.BlockSpec(memory_space=pltpu.VMEM)
    n, _, cols = gathered.shape
    size, groups = drive.shape[0], 4
    with_hole = hole is not None
    arrays = (gathered, hole) if with_hole else (gathered,)
    in_hbm = [pltpu.with_memory_space_constraint(a, pltpu.HBM) for a in arrays]
    in_vmem = (*parts, drive) if with_hole else parts
    out = jax.ShapeDtypeStruct(drive.shape, F32)
    scratch = [pltpu.VMEM((n * size, cols), BF16)]
    if not with_hole:
        out = jax.ShapeDtypeStruct((size + EXPONENT_ROWS, cols), jnp.int16)
        scratch.append(pltpu.VMEM(drive.shape, F32))
    sems = [pltpu.SemaphoreType.DMA((n,))]
    if with_hole:
        scratch.append(pltpu.VMEM((n * size, cols), BF16))
        scratch.append([pltpu.VMEM((size, n * size // groups), BF16) for _ in range(groups)])
        sems += [pltpu.SemaphoreType.DMA((n,)), pltpu.SemaphoreType.DMA((groups,))]
    depth = (2 if with_hole else 1) * n * size
    return pl.pallas_call(
        kernel,
        out_shape=out,
        in_specs=[hbm] * len(in_hbm) + [vmem] * len(in_vmem),
        out_specs=vmem,
        scratch_shapes=scratch + sems,
        compiler_params=pltpu.CompilerParams(vmem_limit_bytes=24 << 20),
        cost_estimate=pl.CostEstimate(
            flops=2 * size * cols * depth, bytes_accessed=4 * size * depth, transcendentals=0
        ),
    )(*in_hbm, *in_vmem)


def body(amplitudes, drive, pair_irrep, occ_irrep, ladder_ints, hole_ints, occ_energy, pair_energy):
    size = amplitudes.shape[0]
    labels = pair_irrep.reshape(-1, LANES)
    partner = [(i, i ^ 1) for i in range(NX)]
    kept = kept_block()
    lent = lax.dynamic_slice_in_dim(ladder_ints, (1 - kept) * size, size)
    lent = lax.ppermute(lent, "x", partner)
    rows = gather_rows(labels, ladder_ints, amplitudes)
    lent_rows = lax.dynamic_slice_in_dim(pair_irrep, (2 * row_rank() + kept) * size, size)
    partner_rank = lax.axis_index("z") * NX + (lax.axis_index("x") ^ 1)
    lent_cols = lax.dynamic_slice_in_dim(pair_irrep, partner_rank * size, size)
    lent = jnp.where(lent_rows[:, None] == lent_cols[None, :], lent, jnp.zeros_like(lent))
    rows = lax.dynamic_update_slice(rows, lent, (2 * size, 0))
    gathered = lax.all_gather(rows, ("y", "core"), axis=0, tiled=False)

    other = lax.ppermute(amplitudes, "x", [(i, NX - 1 - i) for i in range(NX)])
    own = jnp.concatenate([amplitudes, other], axis=1)
    f, b = own, own
    parts = [own]
    for _ in range(NZ // 2 - 1):
        f = lax.ppermute(f, "z", shift(NZ, 1))
        b = lax.ppermute(b, "z", shift(NZ, -1))
        parts += [f, b]
    parts.append(lax.ppermute(f[:, :size], "z", shift(NZ, 1)))
    parts.append(lax.ppermute(b[:, size:], "z", shift(NZ, -1)))

    own_occ = lax.dynamic_slice_in_dim(occ_irrep, row_rank() * size, size)
    hole_kept = jnp.where(
        own_occ[:, None] == occ_irrep[None, :], hole_ints, jnp.zeros_like(hole_ints)
    )
    pair_occ = (occ_energy[:, None] + occ_energy[None, :]).reshape(-1)
    own_energy = lax.dynamic_slice_in_dim(pair_occ, row_rank() * size, size)
    denominator = pair_energy[None, :] - own_energy[:, None]
    for_partner = products(partner_kernel, gathered, None, parts, drive)
    from_partner = lax.ppermute(for_partner, "x", partner)
    scale = jnp.exp2(from_partner[size : size + 1].astype(F32) - FIXED_BITS)
    residual = products(own_kernel, gathered, hole_kept, parts, drive)
    residual = residual + from_partner[:size].astype(F32) * scale
    updated = (amplitudes.astype(F32) - residual / denominator).astype(BF16)
    return residual, updated


def solution(mesh):
    fine = Mesh(mesh.devices.reshape(NY, NCORE, NZ, NX), ("y", "core", "z", "x"))
    row, col = ("y", "core"), ("z", "x")
    in_specs = (
        P(row, col),
        P(row, col),
        P(),
        P(),
        P(row, col),
        P(row, None),
        P(),
        P(col),
    )
    out_specs = (P(row, col), P(row, col))
    return jax.shard_map(body, mesh=fine, in_specs=in_specs, out_specs=out_specs, check_vma=False)
```

```python
import jax
import jax.numpy as jnp
from jax import lax
from jax.experimental import pallas as pl
from jax.experimental.pallas import tpu as pltpu
from jax.sharding import Mesh, PartitionSpec as P

NY, NCORE, NZ, NX = 8, 2, 8, 4
BF16, F32 = jnp.bfloat16, jnp.float32
LANES = 128
FIXED_BITS = 15
FIXED_MOST = 2.0**15 - 1
EXPONENT_ROWS = 16
NEAR = 1024


def shift(n, by):
    return [(i, (i + by) % n) for i in range(n)]


def row_rank():
    return lax.axis_index("y") * NCORE + lax.axis_index("core")


def kept_block():
    x = lax.axis_index("x")
    inner = jnp.logical_or(x == 1, x == 2).astype(jnp.int32)
    return lax.rem(inner + lax.axis_index("core"), 2)


def masked(values, row_labels, col_labels):
    return jnp.where(row_labels == col_labels, values.astype(F32), 0.0).astype(BF16)


def down(line):
    return jnp.broadcast_to(line.astype(F32), (LANES, LANES)).T


def rows_kernel(labels, ladder, amps, out_ref):
    size, cols = amps.shape
    block = kept_block()
    c = lax.axis_index("z") * NX + lax.axis_index("x")
    lines = cols // LANES
    first = (2 * row_rank() + block) * (size // LANES)
    for k in range(size // LANES):
        row_labels = down(labels[pl.ds(first + k, 1), :])
        at = pl.ds(pl.multiple_of(block * size + k * LANES, LANES), LANES)
        for q in range(lines):
            lanes = slice(q * LANES, (q + 1) * LANES)
            col_labels = labels[pl.ds(c * lines + q, 1), :].astype(F32)
            out_ref[k * LANES : (k + 1) * LANES, lanes] = masked(ladder[at, lanes], row_labels, col_labels)
    out_ref[size : 2 * size, :] = amps[...]
    out_ref[2 * size :, :] = jnp.zeros_like(amps)


def gather_rows(labels, ladder, amps):
    vmem = pl.BlockSpec(memory_space=pltpu.VMEM)
    size, cols = amps.shape
    return pl.pallas_call(
        rows_kernel,
        out_shape=jax.ShapeDtypeStruct((3 * size, cols), BF16),
        in_specs=[vmem] * 3,
        out_specs=vmem,
        cost_estimate=pl.CostEstimate(flops=0, bytes_accessed=1 << 20, transcendentals=0),
    )(labels, ladder, amps)


def ladder_copies(gathered, first_row, parts, rows_v, row_sems, size):
    z, x = lax.axis_index("z"), lax.axis_index("x")
    upper = (x >= NX // 2).astype(jnp.int32)
    opposite = lax.rem(z + NZ // 2, NZ)
    sources = [(lax.rem(z + NZ + away, NZ), (0, 1)) for away in (0, -1, 1, -2, 2, -3, 3)]
    sources += [(opposite, (0,)), (opposite, (1,))]
    copies, at = [], 0
    for slot, blocks in sources:
        mine = []
        for j in blocks:
            r = 2 * slot + (upper if j == 0 else 1 - upper)
            src = gathered.at[r, pl.ds(first_row, size)]
            dst = rows_v.at[pl.ds(at, size)]
            mine.append(pltpu.make_async_copy(src, dst, row_sems.at[at // size]))
            at += size
        copies.append(mine)
    return copies


def add_ladder(copies, parts, rows_v, acc, size):
    at = 0
    for part, mine in zip(parts, copies):
        for copy in mine:
            copy.wait()
        depth = size * len(mine)
        acc[...] += jnp.dot(part[...], rows_v[at : at + depth, :], preferred_element_type=F32)
        at += depth


def partner_kernel(gathered, hole, *refs):
    parts, out_ref, near_hole, rows_v, acc, row_sems, hole_sem = refs[:9], *refs[9:]
    size = acc.shape[0]
    copies = ladder_copies(gathered, 2 * size, parts, rows_v, row_sems, size)
    for mine in copies:
        for copy in mine:
            copy.start()
    hole_copy = pltpu.make_async_copy(hole.at[:, pl.ds(0, near_hole.shape[1])], near_hole, hole_sem)
    hole_copy.start()
    acc[...] = jnp.zeros_like(acc)
    add_ladder(copies, parts, rows_v, acc, size)
    largest = jnp.max(jnp.abs(acc[...]), axis=0, keepdims=True)
    exponent = jnp.ceil(jnp.log2(jnp.maximum(largest, 2.0**-100)))
    fixed = jnp.round(acc[...] * jnp.exp2(FIXED_BITS - exponent))
    fixed = jnp.clip(fixed, -FIXED_MOST, FIXED_MOST)
    out_ref[:size, :] = fixed.astype(jnp.int32).astype(jnp.int16)
    rows = out_ref.shape[0] - size
    line = jnp.broadcast_to(exponent, (rows, exponent.shape[1]))
    out_ref[size:, :] = line.astype(jnp.int32).astype(jnp.int16)
    hole_copy.wait()


def own_kernel(gathered, hole, near_hole, *refs):
    parts, drive, out_ref = refs[:9], refs[9], refs[10]
    rows_v, amps_rows_v, hole_v, row_sems, amps_sems, hole_sems = refs[11:]
    n, size = gathered.shape[0], out_ref.shape[0]
    near, width = near_hole.shape[1], hole_v[0].shape[1]
    groups = [near_hole.at[:, pl.ds(at, width)] for at in range(0, near, width)] + list(hole_v)
    per_group = width // size
    hole_copies = []
    for g in range(len(groups)):
        at, mine = g * width, []
        if at >= near:
            i = (at - near) // width
            src = hole.at[:, pl.ds(at, width)]
            mine = [pltpu.make_async_copy(src, groups[g], hole_sems.at[i])]
        for r in range(g * per_group, (g + 1) * per_group):
            src = gathered.at[r, pl.ds(size, size)]
            dst = amps_rows_v.at[pl.ds(r * size, size)]
            mine.append(pltpu.make_async_copy(src, dst, amps_sems.at[r]))
        hole_copies.append(mine)
    copies = ladder_copies(gathered, 0, parts, rows_v, row_sems, size)
    for mine in copies + hole_copies:
        for copy in mine:
            copy.start()
    out_ref[...] = drive[...]
    add_ladder(copies, parts, rows_v, out_ref, size)
    for g, mine in enumerate(hole_copies):
        for copy in mine:
            copy.wait()
        at = pl.ds(g * width, width)
        out_ref[...] += jnp.dot(groups[g][...], amps_rows_v[at], preferred_element_type=F32)


def in_hbm(*arrays):
    return [pltpu.with_memory_space_constraint(a, pltpu.HBM) for a in arrays]


def partner_product(gathered, hole, parts):
    hbm = pl.BlockSpec(memory_space=pltpu.HBM)
    vmem = pl.BlockSpec(memory_space=pltpu.VMEM)
    n, _, cols = gathered.shape
    size = hole.shape[0]
    return pl.pallas_call(
        partner_kernel,
        out_shape=(
            jax.ShapeDtypeStruct((size + EXPONENT_ROWS, cols), jnp.int16),
            jax.ShapeDtypeStruct((size, NEAR), BF16),
        ),
        in_specs=[hbm] * 2 + [vmem] * len(parts),
        out_specs=(vmem, vmem),
        scratch_shapes=[
            pltpu.VMEM((n * size, cols), BF16),
            pltpu.VMEM((size, cols), F32),
            pltpu.SemaphoreType.DMA((n,)),
            pltpu.SemaphoreType.DMA,
        ],
        compiler_params=pltpu.CompilerParams(vmem_limit_bytes=24 << 20),
        cost_estimate=pl.CostEstimate(
            flops=2 * size * cols * n * size, bytes_accessed=4 * size * n * size, transcendentals=0
        ),
    )(*in_hbm(gathered, hole), *parts)


def own_product(gathered, hole, near_hole, parts, drive):
    hbm = pl.BlockSpec(memory_space=pltpu.HBM)
    vmem = pl.BlockSpec(memory_space=pltpu.VMEM)
    n, _, cols = gathered.shape
    size, width = drive.shape[0], 1024
    groups = (hole.shape[1] - near_hole.shape[1]) // width
    return pl.pallas_call(
        own_kernel,
        out_shape=jax.ShapeDtypeStruct(drive.shape, F32),
        in_specs=[hbm] * 2 + [vmem] * (2 + len(parts)),
        out_specs=vmem,
        scratch_shapes=[
            pltpu.VMEM((n * size, cols), BF16),
            pltpu.VMEM((n * size, cols), BF16),
            [pltpu.VMEM((size, width), BF16) for _ in range(groups)],
            pltpu.SemaphoreType.DMA((n,)),
            pltpu.SemaphoreType.DMA((n,)),
            pltpu.SemaphoreType.DMA((groups,)),
        ],
        compiler_params=pltpu.CompilerParams(vmem_limit_bytes=24 << 20),
        cost_estimate=pl.CostEstimate(
            flops=4 * size * cols * n * size, bytes_accessed=8 * size * n * size, transcendentals=0
        ),
    )(*in_hbm(gathered, hole), near_hole, *parts, drive)


def body(amplitudes, drive, pair_irrep, occ_irrep, ladder_ints, hole_ints, occ_energy, pair_energy):
    size = amplitudes.shape[0]
    labels = pair_irrep.reshape(-1, LANES)
    partner = [(i, i ^ 1) for i in range(NX)]
    kept = kept_block()
    lent = lax.dynamic_slice_in_dim(ladder_ints, (1 - kept) * size, size)
    lent = lax.ppermute(lent, "x", partner)
    rows = gather_rows(labels, ladder_ints, amplitudes)
    lent_rows = lax.dynamic_slice_in_dim(pair_irrep, (2 * row_rank() + kept) * size, size)
    partner_rank = lax.axis_index("z") * NX + (lax.axis_index("x") ^ 1)
    lent_cols = lax.dynamic_slice_in_dim(pair_irrep, partner_rank * size, size)
    lent = jnp.where(lent_rows[:, None] == lent_cols[None, :], lent, jnp.zeros_like(lent))
    rows = lax.dynamic_update_slice(rows, lent, (2 * size, 0))
    gathered = lax.all_gather(rows, ("y", "core"), axis=0, tiled=False)

    other = lax.ppermute(amplitudes, "x", [(i, NX - 1 - i) for i in range(NX)])
    own = jnp.concatenate([amplitudes, other], axis=1)
    f, b = own, own
    parts = [own]
    for _ in range(NZ // 2 - 1):
        f = lax.ppermute(f, "z", shift(NZ, 1))
        b = lax.ppermute(b, "z", shift(NZ, -1))
        parts += [f, b]
    parts.append(lax.ppermute(f[:, :size], "z", shift(NZ, 1)))
    parts.append(lax.ppermute(b[:, size:], "z", shift(NZ, -1)))

    own_occ = lax.dynamic_slice_in_dim(occ_irrep, row_rank() * size, size)
    hole_kept = jnp.where(
        own_occ[:, None] == occ_irrep[None, :], hole_ints, jnp.zeros_like(hole_ints)
    )
    pair_occ = (occ_energy[:, None] + occ_energy[None, :]).reshape(-1)
    own_energy = lax.dynamic_slice_in_dim(pair_occ, row_rank() * size, size)
    denominator = pair_energy[None, :] - own_energy[:, None]
    for_partner, near_hole = partner_product(gathered, hole_kept, parts)
    from_partner = lax.ppermute(for_partner, "x", partner)
    scale = jnp.exp2(from_partner[size : size + 1].astype(F32) - FIXED_BITS)
    residual = own_product(gathered, hole_kept, near_hole, parts, drive)
    residual = residual + from_partner[:size].astype(F32) * scale
    updated = (amplitudes.astype(F32) - residual / denominator).astype(BF16)
    return residual, updated


def solution(mesh):
    fine = Mesh(mesh.devices.reshape(NY, NCORE, NZ, NX), ("y", "core", "z", "x"))
    row, col = ("y", "core"), ("z", "x")
    in_specs = (
        P(row, col),
        P(row, col),
        P(),
        P(),
        P(row, col),
        P(row, None),
        P(),
        P(col),
    )
    out_specs = (P(row, col), P(row, col))
    return jax.shard_map(body, mesh=fine, in_specs=in_specs, out_specs=out_specs, check_vma=False)
```

```python
import jax
import jax.numpy as jnp
from jax import lax
from jax.experimental import pallas as pl
from jax.experimental.pallas import tpu as pltpu
from jax.sharding import Mesh, PartitionSpec as P

NY, NCORE, NZ, NX = 8, 2, 8, 4
BF16, F32 = jnp.bfloat16, jnp.float32
LANES = 128
FIXED_BITS = 15
FIXED_MOST = 2.0**15 - 1
EXPONENT_ROWS = 16
NEAR = 1024


def shift(n, by):
    return [(i, (i + by) % n) for i in range(n)]


def row_rank():
    return lax.axis_index("y") * NCORE + lax.axis_index("core")


def kept_block():
    x = lax.axis_index("x")
    inner = jnp.logical_or(x == 1, x == 2).astype(jnp.int32)
    return lax.rem(inner + lax.axis_index("core"), 2)


def masked(values, row_labels, col_labels):
    return jnp.where(row_labels == col_labels, values.astype(F32), 0.0).astype(BF16)


def down(line):
    return jnp.broadcast_to(line.astype(F32), (LANES, LANES)).T


def rows_kernel(labels, ladder, amps, out_ref):
    size, cols = amps.shape
    block = kept_block()
    c = lax.axis_index("z") * NX + lax.axis_index("x")
    lines = cols // LANES
    first = (2 * row_rank() + block) * (size // LANES)
    for k in range(size // LANES):
        row_labels = down(labels[pl.ds(first + k, 1), :])
        at = pl.ds(pl.multiple_of(block * size + k * LANES, LANES), LANES)
        for q in range(lines):
            lanes = slice(q * LANES, (q + 1) * LANES)
            col_labels = labels[pl.ds(c * lines + q, 1), :].astype(F32)
            out_ref[k * LANES : (k + 1) * LANES, lanes] = masked(ladder[at, lanes], row_labels, col_labels)
    out_ref[size : 2 * size, :] = amps[...]
    out_ref[2 * size :, :] = jnp.zeros_like(amps)


def gather_rows(labels, ladder, amps):
    vmem = pl.BlockSpec(memory_space=pltpu.VMEM)
    size, cols = amps.shape
    return pl.pallas_call(
        rows_kernel,
        out_shape=jax.ShapeDtypeStruct((3 * size, cols), BF16),
        in_specs=[vmem] * 3,
        out_specs=vmem,
        cost_estimate=pl.CostEstimate(flops=0, bytes_accessed=1 << 20, transcendentals=0),
    )(labels, ladder, amps)


def ladder_copies(gathered, first_row, parts, rows_v, row_sems, size):
    z, x = lax.axis_index("z"), lax.axis_index("x")
    upper = (x >= NX // 2).astype(jnp.int32)
    opposite = lax.rem(z + NZ // 2, NZ)
    sources = [(lax.rem(z + NZ + away, NZ), (0, 1)) for away in (0, -1, 1, -2, 2, -3, 3)]
    sources += [(opposite, (0,)), (opposite, (1,))]
    copies, at = [], 0
    for slot, blocks in sources:
        mine = []
        for j in blocks:
            r = 2 * slot + (upper if j == 0 else 1 - upper)
            src = gathered.at[r, pl.ds(first_row, size)]
            dst = rows_v.at[pl.ds(at, size)]
            mine.append(pltpu.make_async_copy(src, dst, row_sems.at[at // size]))
            at += size
        copies.append(mine)
    return copies


def add_ladder(copies, parts, rows_v, acc, size):
    at = 0
    for part, mine in zip(parts, copies):
        for copy in mine:
            copy.wait()
        depth = size * len(mine)
        acc[...] += jnp.dot(part[...], rows_v[at : at + depth, :], preferred_element_type=F32)
        at += depth


def partner_kernel(gathered, hole, *refs):
    parts, out_ref, near_hole, rows_v, acc, row_sems, hole_sem = refs[:9], *refs[9:]
    size, cols = acc.shape
    z = lax.axis_index("z")
    upper = (lax.axis_index("x") >= NX // 2).astype(jnp.int32)
    halves = 1
    copies = []
    for h in range(halves):
        for i, away in enumerate((0, -1, 1, -2, 2, -3, 3, NZ // 2)):
            slot = lax.rem(z + NZ + away, NZ)
            src = gathered.at[pl.ds(2 * slot, 2), pl.ds(2 * size, size), pl.ds(h * cols, cols)]
            copies.append(pltpu.make_async_copy(src, rows_v.at[h, i], row_sems.at[h * NZ + i]))
            copies[-1].start()
    hole_copy = pltpu.make_async_copy(hole.at[:, pl.ds(0, near_hole.shape[1])], near_hole, hole_sem)
    hole_copy.start()
    blocks = [(p, i, p, i) for p in range(NZ - 1) for i in range(2)]
    blocks += [(NZ - 1, 0, NZ - 1, 0), (NZ, 0, NZ - 1, 1)]
    extra = out_ref.shape[0] - size
    for h in range(halves):
        lanes = slice(h * cols, (h + 1) * cols)
        acc[:, lanes] = jnp.zeros((size, cols), F32)
        for p, i, chunk, j in blocks:
            if j == 0:
                copies[h * NZ + chunk].wait()
            row = upper if j == 0 else 1 - upper
            acc[:, lanes] += jnp.dot(
                parts[p][:, i * size : (i + 1) * size],
                rows_v[h, chunk, row],
                preferred_element_type=F32,
            )
        sums = acc[:, lanes]
        largest = jnp.max(jnp.abs(sums), axis=0, keepdims=True)
        exponent = jnp.ceil(jnp.log2(jnp.maximum(largest, 2.0**-100)))
        fixed = jnp.round(sums * jnp.exp2(FIXED_BITS - exponent))
        fixed = jnp.clip(fixed, -FIXED_MOST, FIXED_MOST)
        out_ref[:size, lanes] = fixed.astype(jnp.int32).astype(jnp.int16)
        line = jnp.broadcast_to(exponent, (extra, cols))
        out_ref[size:, lanes] = line.astype(jnp.int32).astype(jnp.int16)
    hole_copy.wait()


def own_kernel(gathered, hole, near_hole, *refs):
    parts, drive, out_ref = refs[:9], refs[9], refs[10]
    rows_v, amps_rows_v, hole_v, row_sems, amps_sems, hole_sems = refs[11:]
    n, size = gathered.shape[0], out_ref.shape[0]
    near, width = near_hole.shape[1], hole_v[0].shape[1]
    groups = [near_hole.at[:, pl.ds(at, width)] for at in range(0, near, width)] + list(hole_v)
    per_group = width // size
    hole_copies = []
    for g in range(len(groups)):
        at, mine = g * width, []
        if at >= near:
            i = (at - near) // width
            src = hole.at[:, pl.ds(at, width)]
            mine = [pltpu.make_async_copy(src, groups[g], hole_sems.at[i])]
        for r in range(g * per_group, (g + 1) * per_group):
            src = gathered.at[r, pl.ds(size, size)]
            dst = amps_rows_v.at[pl.ds(r * size, size)]
            mine.append(pltpu.make_async_copy(src, dst, amps_sems.at[r]))
        hole_copies.append(mine)
    copies = ladder_copies(gathered, 0, parts, rows_v, row_sems, size)
    for mine in copies + hole_copies:
        for copy in mine:
            copy.start()
    out_ref[...] = drive[...]
    add_ladder(copies, parts, rows_v, out_ref, size)
    for g, mine in enumerate(hole_copies):
        for copy in mine:
            copy.wait()
        at = pl.ds(g * width, width)
        out_ref[...] += jnp.dot(groups[g][...], amps_rows_v[at], preferred_element_type=F32)


def in_hbm(*arrays):
    return [pltpu.with_memory_space_constraint(a, pltpu.HBM) for a in arrays]


def partner_product(gathered, hole, parts):
    hbm = pl.BlockSpec(memory_space=pltpu.HBM)
    vmem = pl.BlockSpec(memory_space=pltpu.VMEM)
    n, _, cols = gathered.shape
    size = hole.shape[0]
    return pl.pallas_call(
        partner_kernel,
        out_shape=(
            jax.ShapeDtypeStruct((size + EXPONENT_ROWS, cols), jnp.int16),
            jax.ShapeDtypeStruct((size, NEAR), BF16),
        ),
        in_specs=[hbm] * 2 + [vmem] * len(parts),
        out_specs=(vmem, vmem),
        scratch_shapes=[
            pltpu.VMEM((1, NZ, 2, size, cols), BF16),
            pltpu.VMEM((size, cols), F32),
            pltpu.SemaphoreType.DMA((NZ,)),
            pltpu.SemaphoreType.DMA,
        ],
        compiler_params=pltpu.CompilerParams(vmem_limit_bytes=24 << 20),
        cost_estimate=pl.CostEstimate(
            flops=2 * size * cols * n * size, bytes_accessed=4 * size * n * size, transcendentals=0
        ),
    )(*in_hbm(gathered, hole), *parts)


def own_product(gathered, hole, near_hole, parts, drive):
    hbm = pl.BlockSpec(memory_space=pltpu.HBM)
    vmem = pl.BlockSpec(memory_space=pltpu.VMEM)
    n, _, cols = gathered.shape
    size, width = drive.shape[0], 1024
    groups = (hole.shape[1] - near_hole.shape[1]) // width
    return pl.pallas_call(
        own_kernel,
        out_shape=jax.ShapeDtypeStruct(drive.shape, F32),
        in_specs=[hbm] * 2 + [vmem] * (2 + len(parts)),
        out_specs=vmem,
        scratch_shapes=[
            pltpu.VMEM((n * size, cols), BF16),
            pltpu.VMEM((n * size, cols), BF16),
            [pltpu.VMEM((size, width), BF16) for _ in range(groups)],
            pltpu.SemaphoreType.DMA((n,)),
            pltpu.SemaphoreType.DMA((n,)),
            pltpu.SemaphoreType.DMA((groups,)),
        ],
        compiler_params=pltpu.CompilerParams(vmem_limit_bytes=24 << 20),
        cost_estimate=pl.CostEstimate(
            flops=4 * size * cols * n * size, bytes_accessed=8 * size * n * size, transcendentals=0
        ),
    )(*in_hbm(gathered, hole), near_hole, *parts, drive)


def body(amplitudes, drive, pair_irrep, occ_irrep, ladder_ints, hole_ints, occ_energy, pair_energy):
    size = amplitudes.shape[0]
    labels = pair_irrep.reshape(-1, LANES)
    partner = [(i, i ^ 1) for i in range(NX)]
    kept = kept_block()
    lent = lax.dynamic_slice_in_dim(ladder_ints, (1 - kept) * size, size)
    lent = lax.ppermute(lent, "x", partner)
    rows = gather_rows(labels, ladder_ints, amplitudes)
    lent_rows = lax.dynamic_slice_in_dim(pair_irrep, (2 * row_rank() + kept) * size, size)
    partner_rank = lax.axis_index("z") * NX + (lax.axis_index("x") ^ 1)
    lent_cols = lax.dynamic_slice_in_dim(pair_irrep, partner_rank * size, size)
    lent = jnp.where(lent_rows[:, None] == lent_cols[None, :], lent, jnp.zeros_like(lent))
    rows = lax.dynamic_update_slice(rows, lent, (2 * size, 0))
    gathered = lax.all_gather(rows, ("y", "core"), axis=0, tiled=False)

    other = lax.ppermute(amplitudes, "x", [(i, NX - 1 - i) for i in range(NX)])
    own = jnp.concatenate([amplitudes, other], axis=1)
    f, b = own, own
    parts = [own]
    for _ in range(NZ // 2 - 1):
        f = lax.ppermute(f, "z", shift(NZ, 1))
        b = lax.ppermute(b, "z", shift(NZ, -1))
        parts += [f, b]
    parts.append(lax.ppermute(f[:, :size], "z", shift(NZ, 1)))
    parts.append(lax.ppermute(b[:, size:], "z", shift(NZ, -1)))

    own_occ = lax.dynamic_slice_in_dim(occ_irrep, row_rank() * size, size)
    hole_kept = jnp.where(
        own_occ[:, None] == occ_irrep[None, :], hole_ints, jnp.zeros_like(hole_ints)
    )
    pair_occ = (occ_energy[:, None] + occ_energy[None, :]).reshape(-1)
    own_energy = lax.dynamic_slice_in_dim(pair_occ, row_rank() * size, size)
    denominator = pair_energy[None, :] - own_energy[:, None]
    for_partner, near_hole = partner_product(gathered, hole_kept, parts)
    from_partner = lax.ppermute(for_partner, "x", partner)
    scale = jnp.exp2(from_partner[size : size + 1].astype(F32) - FIXED_BITS)
    residual = own_product(gathered, hole_kept, near_hole, parts, drive)
    residual = residual + from_partner[:size].astype(F32) * scale
    updated = (amplitudes.astype(F32) - residual / denominator).astype(BF16)
    return residual, updated


def solution(mesh):
    fine = Mesh(mesh.devices.reshape(NY, NCORE, NZ, NX), ("y", "core", "z", "x"))
    row, col = ("y", "core"), ("z", "x")
    in_specs = (
        P(row, col),
        P(row, col),
        P(),
        P(),
        P(row, col),
        P(row, None),
        P(),
        P(col),
    )
    out_specs = (P(row, col), P(row, col))
    return jax.shard_map(body, mesh=fine, in_specs=in_specs, out_specs=out_specs, check_vma=False)
```

```python
import jax
import jax.numpy as jnp
from jax import lax
from jax.experimental import pallas as pl
from jax.experimental.pallas import tpu as pltpu
from jax.sharding import Mesh, PartitionSpec as P

NY, NCORE, NZ, NX = 8, 2, 8, 4
BF16, F32 = jnp.bfloat16, jnp.float32
LANES = 128
FIXED_BITS = 15
FIXED_MOST = 2.0**15 - 1
EXPONENT_ROWS = 16


def shift(n, by):
    return [(i, (i + by) % n) for i in range(n)]


def row_rank():
    return lax.axis_index("y") * NCORE + lax.axis_index("core")


def kept_block():
    x = lax.axis_index("x")
    inner = jnp.logical_or(x == 1, x == 2).astype(jnp.int32)
    return lax.rem(inner + lax.axis_index("core"), 2)


def masked(values, row_labels, col_labels):
    return jnp.where(row_labels == col_labels, values.astype(F32), 0.0).astype(BF16)


def down(line):
    return jnp.broadcast_to(line.astype(F32), (LANES, LANES)).T


def rows_kernel(labels, ladder, amps, out_ref):
    size, cols = amps.shape
    block = kept_block()
    c = lax.axis_index("z") * NX + lax.axis_index("x")
    lines = cols // LANES
    first = (2 * row_rank() + block) * (size // LANES)
    for k in range(size // LANES):
        row_labels = down(labels[pl.ds(first + k, 1), :])
        at = pl.ds(pl.multiple_of(block * size + k * LANES, LANES), LANES)
        for q in range(lines):
            lanes = slice(q * LANES, (q + 1) * LANES)
            col_labels = labels[pl.ds(c * lines + q, 1), :].astype(F32)
            out_ref[k * LANES : (k + 1) * LANES, lanes] = masked(ladder[at, lanes], row_labels, col_labels)
    out_ref[size : 2 * size, :] = amps[...]
    out_ref[2 * size :, :] = jnp.zeros_like(amps)


def gather_rows(labels, ladder, amps):
    vmem = pl.BlockSpec(memory_space=pltpu.VMEM)
    size, cols = amps.shape
    return pl.pallas_call(
        rows_kernel,
        out_shape=jax.ShapeDtypeStruct((3 * size, cols), BF16),
        in_specs=[vmem] * 3,
        out_specs=vmem,
        cost_estimate=pl.CostEstimate(flops=0, bytes_accessed=1 << 20, transcendentals=0),
    )(labels, ladder, amps)


def ladder_copies(gathered, first_row, parts, rows_v, row_sems, size):
    z, x = lax.axis_index("z"), lax.axis_index("x")
    upper = (x >= NX // 2).astype(jnp.int32)
    opposite = lax.rem(z + NZ // 2, NZ)
    sources = [(lax.rem(z + NZ + away, NZ), (0, 1)) for away in (0, -1, 1, -2, 2, -3, 3)]
    sources += [(opposite, (0,)), (opposite, (1,))]
    copies, at = [], 0
    for slot, blocks in sources:
        mine = []
        for j in blocks:
            r = 2 * slot + (upper if j == 0 else 1 - upper)
            src = gathered.at[r, pl.ds(first_row, size)]
            dst = rows_v.at[pl.ds(at, size)]
            mine.append(pltpu.make_async_copy(src, dst, row_sems.at[at // size]))
            at += size
        copies.append(mine)
    return copies


def add_ladder(copies, parts, rows_v, acc, size):
    at = 0
    for part, mine in zip(parts, copies):
        for copy in mine:
            copy.wait()
        depth = size * len(mine)
        acc[...] += jnp.dot(part[...], rows_v[at : at + depth, :], preferred_element_type=F32)
        at += depth


def partner_kernel(gathered, *refs):
    parts, out_ref, rows_v, acc, row_sems = refs[:9], *refs[9:]
    size = acc.shape[0]
    copies = ladder_copies(gathered, 2 * size, parts, rows_v, row_sems, size)
    for mine in copies:
        for copy in mine:
            copy.start()
    acc[...] = jnp.zeros_like(acc)
    add_ladder(copies, parts, rows_v, acc, size)
    largest = jnp.max(jnp.abs(acc[...]), axis=0, keepdims=True)
    exponent = jnp.ceil(jnp.log2(jnp.maximum(largest, 2.0**-100)))
    fixed = jnp.round(acc[...] * jnp.exp2(FIXED_BITS - exponent))
    fixed = jnp.clip(fixed, -FIXED_MOST, FIXED_MOST)
    out_ref[:size, :] = fixed.astype(jnp.int32).astype(jnp.int16)
    rows = out_ref.shape[0] - size
    line = jnp.broadcast_to(exponent, (rows, exponent.shape[1]))
    out_ref[size:, :] = line.astype(jnp.int32).astype(jnp.int16)


def own_kernel(gathered, hole, *refs):
    parts, drive, out_ref = refs[:9], refs[9], refs[10]
    rows_v, amps_rows_v, hole_v, row_sems, amps_sems, hole_sems = refs[11:]
    n, size = gathered.shape[0], out_ref.shape[0]
    group = n // len(hole_v)
    hole_copies = []
    for g in range(len(hole_v)):
        src = hole.at[:, pl.ds(g * group * size, group * size)]
        mine = [pltpu.make_async_copy(src, hole_v[g], hole_sems.at[g])]
        for r in range(g * group, (g + 1) * group):
            src = gathered.at[r, pl.ds(size, size)]
            dst = amps_rows_v.at[pl.ds(r * size, size)]
            mine.append(pltpu.make_async_copy(src, dst, amps_sems.at[r]))
        hole_copies.append(mine)
    copies = ladder_copies(gathered, 0, parts, rows_v, row_sems, size)
    for mine in copies + hole_copies:
        for copy in mine:
            copy.start()
    out_ref[...] = drive[...]
    add_ladder(copies, parts, rows_v, out_ref, size)
    for g, mine in enumerate(hole_copies):
        for copy in mine:
            copy.wait()
        at = pl.ds(g * group * size, group * size)
        out_ref[...] += jnp.dot(hole_v[g][...], amps_rows_v[at], preferred_element_type=F32)


def products(kernel, gathered, hole, parts, drive):
    hbm = pl.BlockSpec(memory_space=pltpu.HBM)
    vmem = pl.BlockSpec(memory_space=pltpu.VMEM)
    n, _, cols = gathered.shape
    size, groups = drive.shape[0], 4
    with_hole = hole is not None
    arrays = (gathered, hole) if with_hole else (gathered,)
    in_hbm = [pltpu.with_memory_space_constraint(a, pltpu.HBM) for a in arrays]
    in_vmem = (*parts, drive) if with_hole else parts
    out = jax.ShapeDtypeStruct(drive.shape, F32)
    scratch = [pltpu.VMEM((n * size, cols), BF16)]
    if not with_hole:
        out = jax.ShapeDtypeStruct((size + EXPONENT_ROWS, cols), jnp.int16)
        scratch.append(pltpu.VMEM(drive.shape, F32))
    sems = [pltpu.SemaphoreType.DMA((n,))]
    if with_hole:
        scratch.append(pltpu.VMEM((n * size, cols), BF16))
        scratch.append([pltpu.VMEM((size, n * size // groups), BF16) for _ in range(groups)])
        sems += [pltpu.SemaphoreType.DMA((n,)), pltpu.SemaphoreType.DMA((groups,))]
    depth = (2 if with_hole else 1) * n * size
    return pl.pallas_call(
        kernel,
        out_shape=out,
        in_specs=[hbm] * len(in_hbm) + [vmem] * len(in_vmem),
        out_specs=vmem,
        scratch_shapes=scratch + sems,
        compiler_params=pltpu.CompilerParams(vmem_limit_bytes=24 << 20),
        cost_estimate=pl.CostEstimate(
            flops=2 * size * cols * depth, bytes_accessed=4 * size * depth, transcendentals=0
        ),
    )(*in_hbm, *in_vmem)


def body(amplitudes, drive, pair_irrep, occ_irrep, ladder_ints, hole_ints, occ_energy, pair_energy):
    size = amplitudes.shape[0]
    labels = pair_irrep.reshape(-1, LANES)
    partner = [(i, i ^ 1) for i in range(NX)]
    kept = kept_block()
    lent = lax.dynamic_slice_in_dim(ladder_ints, (1 - kept) * size, size)
    lent = lax.ppermute(lent, "x", partner)
    rows = gather_rows(labels, ladder_ints, amplitudes)
    lent_rows = lax.dynamic_slice_in_dim(pair_irrep, (2 * row_rank() + kept) * size, size)
    partner_rank = lax.axis_index("z") * NX + (lax.axis_index("x") ^ 1)
    lent_cols = lax.dynamic_slice_in_dim(pair_irrep, partner_rank * size, size)
    lent = jnp.where(lent_rows[:, None] == lent_cols[None, :], lent, jnp.zeros_like(lent))
    rows = lax.dynamic_update_slice(rows, lent, (2 * size, 0))
    gathered = lax.all_gather(rows, ("y", "core"), axis=0, tiled=False)

    other = lax.ppermute(amplitudes, "x", [(i, NX - 1 - i) for i in range(NX)])
    own = jnp.concatenate([amplitudes, other], axis=1)
    f, b = own, own
    parts = [own]
    for _ in range(NZ // 2 - 1):
        f = lax.ppermute(f, "z", shift(NZ, 1))
        b = lax.ppermute(b, "z", shift(NZ, -1))
        parts += [f, b]
    parts.append(lax.ppermute(f[:, :size], "z", shift(NZ, 1)))
    parts.append(lax.ppermute(b[:, size:], "z", shift(NZ, -1)))

    own_occ = lax.dynamic_slice_in_dim(occ_irrep, row_rank() * size, size)
    hole_kept = jnp.where(
        own_occ[:, None] == occ_irrep[None, :], hole_ints, jnp.zeros_like(hole_ints)
    )
    span = size // occ_energy.shape[0]
    outer = lax.dynamic_slice_in_dim(occ_energy, row_rank() * span, span)
    own_energy = (outer[:, None] + occ_energy[None, :]).reshape(-1)
    denominator = pair_energy[None, :] - own_energy[:, None]
    for_partner = products(partner_kernel, gathered, None, parts, drive)
    from_partner = lax.ppermute(for_partner, "x", partner)
    scale = jnp.exp2(from_partner[size : size + 1].astype(F32) - FIXED_BITS)
    residual = products(own_kernel, gathered, hole_kept, parts, drive)
    residual = residual + from_partner[:size].astype(F32) * scale
    updated = (amplitudes.astype(F32) - residual / denominator).astype(BF16)
    return residual, updated


def solution(mesh):
    fine = Mesh(mesh.devices.reshape(NY, NCORE, NZ, NX), ("y", "core", "z", "x"))
    row, col = ("y", "core"), ("z", "x")
    in_specs = (
        P(row, col),
        P(row, col),
        P(),
        P(),
        P(row, col),
        P(row, None),
        P(),
        P(col),
    )
    out_specs = (P(row, col), P(row, col))
    return jax.shard_map(body, mesh=fine, in_specs=in_specs, out_specs=out_specs, check_vma=False)
```

```python
import jax
import jax.numpy as jnp
from jax import lax
from jax.experimental import pallas as pl
from jax.experimental.pallas import tpu as pltpu
from jax.sharding import Mesh, PartitionSpec as P

NY, NCORE, NZ, NX = 8, 2, 8, 4
BF16, F32 = jnp.bfloat16, jnp.float32
LANES = 128
FIXED_BITS = 15
FIXED_MOST = 2.0**15 - 1
EXPONENT_ROWS = 16


def shift(n, by):
    return [(i, (i + by) % n) for i in range(n)]


def row_rank():
    return lax.axis_index("y") * NCORE + lax.axis_index("core")


def kept_block():
    x = lax.axis_index("x")
    inner = jnp.logical_or(x == 1, x == 2).astype(jnp.int32)
    return lax.rem(inner + lax.axis_index("core"), 2)


def masked(values, row_labels, col_labels):
    return jnp.where(row_labels == col_labels, values.astype(F32), 0.0).astype(BF16)


def down(line):
    return jnp.broadcast_to(line.astype(F32), (LANES, LANES)).T


def rows_kernel(labels, ladder, amps, out_ref):
    size, cols = amps.shape
    block = kept_block()
    c = lax.axis_index("z") * NX + lax.axis_index("x")
    lines = cols // LANES
    first = (2 * row_rank() + block) * (size // LANES)
    for k in range(size // LANES):
        row_labels = down(labels[pl.ds(first + k, 1), :])
        at = pl.ds(pl.multiple_of(block * size + k * LANES, LANES), LANES)
        for q in range(lines):
            lanes = slice(q * LANES, (q + 1) * LANES)
            col_labels = labels[pl.ds(c * lines + q, 1), :].astype(F32)
            out_ref[k * LANES : (k + 1) * LANES, lanes] = masked(ladder[at, lanes], row_labels, col_labels)
    out_ref[size : 2 * size, :] = amps[...]
    out_ref[2 * size :, :] = jnp.zeros_like(amps)


def gather_rows(labels, ladder, amps):
    vmem = pl.BlockSpec(memory_space=pltpu.VMEM)
    size, cols = amps.shape
    return pl.pallas_call(
        rows_kernel,
        out_shape=jax.ShapeDtypeStruct((3 * size, cols), BF16),
        in_specs=[vmem] * 3,
        out_specs=vmem,
        cost_estimate=pl.CostEstimate(flops=0, bytes_accessed=1 << 20, transcendentals=0),
    )(labels, ladder, amps)


def ladder_copies(gathered, first_row, parts, rows_v, row_sems, size):
    z, x = lax.axis_index("z"), lax.axis_index("x")
    upper = (x >= NX // 2).astype(jnp.int32)
    opposite = lax.rem(z + NZ // 2, NZ)
    sources = [(lax.rem(z + NZ + away, NZ), (0, 1)) for away in (0, -1, 1, -2, 2, -3, 3)]
    sources += [(opposite, (0,)), (opposite, (1,))]
    copies, at = [], 0
    for slot, blocks in sources:
        mine = []
        for j in blocks:
            r = 2 * slot + (upper if j == 0 else 1 - upper)
            src = gathered.at[r, pl.ds(first_row, size)]
            dst = rows_v.at[pl.ds(at, size)]
            mine.append(pltpu.make_async_copy(src, dst, row_sems.at[at // size]))
            at += size
        copies.append(mine)
    return copies


def add_ladder(copies, parts, rows_v, acc, size):
    at = 0
    for part, mine in zip(parts, copies):
        for copy in mine:
            copy.wait()
        depth = size * len(mine)
        acc[...] += jnp.dot(part[...], rows_v[at : at + depth, :], preferred_element_type=F32)
        at += depth


def partner_kernel(gathered, *refs):
    parts, out_ref, rows_v, acc, row_sems = refs[:9], *refs[9:]
    size = acc.shape[0]
    z = lax.axis_index("z")
    upper = (lax.axis_index("x") >= NX // 2).astype(jnp.int32)
    copies = []
    for i, away in enumerate((0, -1, 1, -2, 2, -3, 3, NZ // 2)):
        src = gathered.at[pl.ds(2 * lax.rem(z + NZ + away, NZ), 2), pl.ds(2 * size, size)]
        dst = rows_v.at[pl.ds(2 * i, 2)]
        copies.append(pltpu.make_async_copy(src, dst, row_sems.at[i]))
        copies[-1].start()
    acc[...] = jnp.zeros_like(acc)
    blocks = [(p, i, p, i) for p in range(NZ - 1) for i in range(2)]
    blocks += [(NZ - 1, 0, NZ - 1, 0), (NZ, 0, NZ - 1, 1)]
    for p, i, chunk, j in blocks:
        if j == 0:
            copies[chunk].wait()
        part = parts[p][:, i * size : (i + 1) * size]
        row = upper if j == 0 else 1 - upper
        acc[...] += jnp.dot(part, rows_v[2 * chunk + row], preferred_element_type=F32)
    largest = jnp.max(jnp.abs(acc[...]), axis=0, keepdims=True)
    exponent = jnp.ceil(jnp.log2(jnp.maximum(largest, 2.0**-100)))
    fixed = jnp.round(acc[...] * jnp.exp2(FIXED_BITS - exponent))
    fixed = jnp.clip(fixed, -FIXED_MOST, FIXED_MOST)
    out_ref[:size, :] = fixed.astype(jnp.int32).astype(jnp.int16)
    rows = out_ref.shape[0] - size
    line = jnp.broadcast_to(exponent, (rows, exponent.shape[1]))
    out_ref[size:, :] = line.astype(jnp.int32).astype(jnp.int16)


def own_kernel(gathered, hole, *refs):
    parts, drive, out_ref = refs[:9], refs[9], refs[10]
    rows_v, amps_rows_v, hole_v, row_sems, amps_sems, hole_sems = refs[11:]
    n, size = gathered.shape[0], out_ref.shape[0]
    group = n // len(hole_v)
    hole_copies = []
    for g in range(len(hole_v)):
        src = hole.at[:, pl.ds(g * group * size, group * size)]
        mine = [pltpu.make_async_copy(src, hole_v[g], hole_sems.at[g])]
        for r in range(g * group, (g + 1) * group):
            src = gathered.at[r, pl.ds(size, size)]
            dst = amps_rows_v.at[pl.ds(r * size, size)]
            mine.append(pltpu.make_async_copy(src, dst, amps_sems.at[r]))
        hole_copies.append(mine)
    copies = ladder_copies(gathered, 0, parts, rows_v, row_sems, size)
    for mine in copies + hole_copies:
        for copy in mine:
            copy.start()
    out_ref[...] = drive[...]
    add_ladder(copies, parts, rows_v, out_ref, size)
    for g, mine in enumerate(hole_copies):
        for copy in mine:
            copy.wait()
        at = pl.ds(g * group * size, group * size)
        out_ref[...] += jnp.dot(hole_v[g][...], amps_rows_v[at], preferred_element_type=F32)


def products(kernel, gathered, hole, parts, drive):
    hbm = pl.BlockSpec(memory_space=pltpu.HBM)
    vmem = pl.BlockSpec(memory_space=pltpu.VMEM)
    n, _, cols = gathered.shape
    size, groups = drive.shape[0], 4
    with_hole = hole is not None
    arrays = (gathered, hole) if with_hole else (gathered,)
    in_hbm = [pltpu.with_memory_space_constraint(a, pltpu.HBM) for a in arrays]
    in_vmem = (*parts, drive) if with_hole else parts
    out = jax.ShapeDtypeStruct(drive.shape, F32)
    shape = (n * size, cols) if with_hole else (n, size, cols)
    scratch = [pltpu.VMEM(shape, BF16)]
    if not with_hole:
        out = jax.ShapeDtypeStruct((size + EXPONENT_ROWS, cols), jnp.int16)
        scratch.append(pltpu.VMEM(drive.shape, F32))
    sems = [pltpu.SemaphoreType.DMA((n,))]
    if with_hole:
        scratch.append(pltpu.VMEM((n * size, cols), BF16))
        scratch.append([pltpu.VMEM((size, n * size // groups), BF16) for _ in range(groups)])
        sems += [pltpu.SemaphoreType.DMA((n,)), pltpu.SemaphoreType.DMA((groups,))]
    depth = (2 if with_hole else 1) * n * size
    return pl.pallas_call(
        kernel,
        out_shape=out,
        in_specs=[hbm] * len(in_hbm) + [vmem] * len(in_vmem),
        out_specs=vmem,
        scratch_shapes=scratch + sems,
        compiler_params=pltpu.CompilerParams(vmem_limit_bytes=24 << 20),
        cost_estimate=pl.CostEstimate(
            flops=2 * size * cols * depth, bytes_accessed=4 * size * depth, transcendentals=0
        ),
    )(*in_hbm, *in_vmem)


def body(amplitudes, drive, pair_irrep, occ_irrep, ladder_ints, hole_ints, occ_energy, pair_energy):
    size = amplitudes.shape[0]
    labels = pair_irrep.reshape(-1, LANES)
    partner = [(i, i ^ 1) for i in range(NX)]
    kept = kept_block()
    lent = lax.dynamic_slice_in_dim(ladder_ints, (1 - kept) * size, size)
    lent = lax.ppermute(lent, "x", partner)
    rows = gather_rows(labels, ladder_ints, amplitudes)
    lent_rows = lax.dynamic_slice_in_dim(pair_irrep, (2 * row_rank() + kept) * size, size)
    partner_rank = lax.axis_index("z") * NX + (lax.axis_index("x") ^ 1)
    lent_cols = lax.dynamic_slice_in_dim(pair_irrep, partner_rank * size, size)
    lent = jnp.where(lent_rows[:, None] == lent_cols[None, :], lent, jnp.zeros_like(lent))
    rows = lax.dynamic_update_slice(rows, lent, (2 * size, 0))
    gathered = lax.all_gather(rows, ("y", "core"), axis=0, tiled=False)

    other = lax.ppermute(amplitudes, "x", [(i, NX - 1 - i) for i in range(NX)])
    own = jnp.concatenate([amplitudes, other], axis=1)
    f, b = own, own
    parts = [own]
    for _ in range(NZ // 2 - 1):
        f = lax.ppermute(f, "z", shift(NZ, 1))
        b = lax.ppermute(b, "z", shift(NZ, -1))
        parts += [f, b]
    parts.append(lax.ppermute(f[:, :size], "z", shift(NZ, 1)))
    parts.append(lax.ppermute(b[:, size:], "z", shift(NZ, -1)))

    own_occ = lax.dynamic_slice_in_dim(occ_irrep, row_rank() * size, size)
    hole_kept = jnp.where(
        own_occ[:, None] == occ_irrep[None, :], hole_ints, jnp.zeros_like(hole_ints)
    )
    pair_occ = (occ_energy[:, None] + occ_energy[None, :]).reshape(-1)
    own_energy = lax.dynamic_slice_in_dim(pair_occ, row_rank() * size, size)
    denominator = pair_energy[None, :] - own_energy[:, None]
    for_partner = products(partner_kernel, gathered, None, parts, drive)
    from_partner = lax.ppermute(for_partner, "x", partner)
    scale = jnp.exp2(from_partner[size : size + 1].astype(F32) - FIXED_BITS)
    residual = products(own_kernel, gathered, hole_kept, parts, drive)
    residual = residual + from_partner[:size].astype(F32) * scale
    updated = (amplitudes.astype(F32) - residual / denominator).astype(BF16)
    return residual, updated


def solution(mesh):
    fine = Mesh(mesh.devices.reshape(NY, NCORE, NZ, NX), ("y", "core", "z", "x"))
    row, col = ("y", "core"), ("z", "x")
    in_specs = (
        P(row, col),
        P(row, col),
        P(),
        P(),
        P(row, col),
        P(row, None),
        P(),
        P(col),
    )
    out_specs = (P(row, col), P(row, col))
    return jax.shard_map(body, mesh=fine, in_specs=in_specs, out_specs=out_specs, check_vma=False)
```
